128 devices in a mesh: dp: 16 (over y, z), tensor: 8 (over x, core).
Axes of the slice: x: 4, y: 4, z: 4, core: 2. Of those that a mesh axis runs over, the one named last changes fastest.
Arguments:
- activations: bfloat16 [16384, 8192], P('dp'), may hold values from -6 to 6
- output_grads: bfloat16 [2, 16384, 1024], P(None, 'dp', 'tensor'), may hold values from -0.1875 to 0.1875
- error_feedback: bfloat16 [2, 16, 8192, 1024], P(None, 'dp', None, 'tensor'), may hold values from -3 to 3
- warm_start: float32 [2, 1024, 8], P(None, 'tensor'), may hold values from -6 to 6
Outputs:
- decoded: bfloat16 [2, 8192, 1024], P(None, 'dp', 'tensor')
- new_error: bfloat16 [2, 16, 8192, 1024], P(None, 'dp', None, 'tensor')
The draws below stay inside these ranges and needn't reach their ends.
All inputs are finite; a program needn't handle non-finite values.
Results may differ from the reference program's by a relative error of at most 0.0015.
Values sent between devices are 32-bit elements; how exact they have to be, the bound alone decides.
No kernel may reach another device: no remote copies, remote signals or barrier semaphores. Data moves between devices by JAX's collectives and lax.ppermute only.
A program may use at most 128 MiB of HBM per device.

```python
import jax
import jax.numpy as jnp
from jax import lax

D = 8192
RANK = 8
ITERS = 2
TOK_REP = 1024
REPLICAS = 16
ROWS_ALL = 16384
W_TOTAL = 1024


def levels(key, extent, shards, low, top_value):
    def one(position, blocks):
        draws = jax.random.uniform(jax.random.fold_in(jax.random.fold_in(key, 6), position), (blocks,), jnp.float32, low / len(shards), top_value / len(shards))
        return jnp.repeat(jnp.exp(draws), extent[position] // blocks).reshape((-1,) + (1,) * (len(extent) - position - 1))

    gain = one(*shards[0])
    for cut in shards[1:]:
        gain = gain * one(*cut)
    return gain


def gaussian(stream_key, dims, deviation, bound, shards=(), kind=jnp.bfloat16):
    drawn = deviation * jax.random.normal(stream_key, dims, jnp.float32)
    if shards:
        drawn = drawn * levels(stream_key, dims, shards, -0.22, 0.18)
    return jnp.clip(drawn, -bound, bound).astype(kind)


def setup_inputs(seed: int = 0) -> dict:
    streams_of = jax.random.split(jax.random.key(seed), 5)
    activations = gaussian(streams_of[0], (ROWS_ALL, D), 1.0, 6.0, ((0, 16),))
    output_grads = gaussian(streams_of[1], (2, ROWS_ALL, W_TOTAL), (TOK_REP ** -0.5), 0.1875, ((1, 16), (2, 8)))
    error_feedback = gaussian(streams_of[2], (2, REPLICAS, D, W_TOTAL), 0.5, 3.0, ((1, 16), (3, 8)))
    warm_start = gaussian(streams_of[3], (2, W_TOTAL, RANK), 1.0, 6.0, ((1, 8),), jnp.float32)
    return dict(activations=activations, output_grads=output_grads, error_feedback=error_feedback, warm_start=warm_start)


HIGHEST = lax.Precision.HIGHEST

def lower_inverse(lower_factor):
    order = lower_factor.shape[-1]
    identity = jnp.eye(order, dtype=jnp.float32)
    inverse = jnp.zeros_like(lower_factor)
    for column in range(order):
        known = jnp.einsum('mj,mjk->mk', lower_factor[:, column, :], inverse, precision=HIGHEST)
        next_row = (identity[column][None, :] - known) / lower_factor[:, column, column][:, None]
        inverse = inverse.at[:, column, :].set(next_row)
    return inverse

def orthonormal(summed):
    gram_total = jnp.einsum('dmk,dml->mkl', summed, summed, precision=HIGHEST)
    lower_factor = jnp.linalg.cholesky(gram_total)
    inverse = lower_inverse(lower_factor)
    return jnp.einsum('dmk,mlk->dml', summed, inverse, precision=HIGHEST)

def reference(activations, output_grads, error_feedback, warm_start):
    collected = []
    for replica in range(REPLICAS):
        row_block = activations[replica * TOK_REP:(replica + 1) * TOK_REP]
        grads_block = output_grads[:, replica * TOK_REP:(replica + 1) * TOK_REP]
        products = jnp.stack([jnp.dot(row_block.T.astype(jnp.float32), grads_block[matrix].astype(jnp.float32), preferred_element_type=jnp.float32) for matrix in range(2)])
        collected.append(products + error_feedback[:, replica].astype(jnp.float32))
    updates = jnp.stack(collected, axis=1)
    factor = warm_start
    basis = None
    for iteration in range(ITERS):
        summed = jnp.einsum('mrdw,mwk->dmk', updates, factor, precision=HIGHEST)
        basis = orthonormal(summed)
        factor = jnp.einsum('mrdw,dmk->mwk', updates, basis, precision=HIGHEST)
    mean_update = jnp.einsum('dmk,mwk->mdw', basis, factor, precision=HIGHEST) / REPLICAS
    new_error = (updates - mean_update[:, None]).astype(jnp.bfloat16)
    return (mean_update.astype(jnp.bfloat16), new_error)
```

```python
import functools

import jax
import jax.numpy as jnp
from jax import lax
from jax.experimental import pallas as pl
from jax.experimental.pallas import tpu as pltpu
from jax.sharding import PartitionSpec as P

RANK = 8
LANES = 128
F32, BF16 = jnp.float32, jnp.bfloat16
HIGHEST = lax.Precision.HIGHEST
EVERY = ("dp", "tensor")
NT = (((1,), (1,)), ((), ()))
TN = (((0,), (0,)), ((), ()))


def split(x):
    high = x.astype(BF16)
    return high, (x - high.astype(F32)).astype(BF16)


def dot(x, y, dims=(((1,), (0,)), ((), ()))):
    return lax.dot_general(x, y, dims, preferred_element_type=F32)


def block_diagonal(rows):
    zero = jnp.zeros_like(rows[0])
    top = jnp.concatenate([rows[0], zero], axis=1)
    bottom = jnp.concatenate([zero, rows[1]], axis=1)
    return jnp.concatenate([top, bottom], axis=0)


def left_terms(factor_rows, high, low):
    f_high, f_low = split(factor_rows)
    both = dot(jnp.concatenate([f_high, f_low], axis=0), high)
    return both[:16] + both[16:] + dot(f_high, low)


def store_tiles(out_ref, terms):
    for m in range(2):
        for b in range(terms.shape[1] // LANES):
            out_ref[m, b] = terms[m * RANK : (m + 1) * RANK, b * LANES : (b + 1) * LANES]


def rows_of(tiles_ref, m):
    return jnp.concatenate([tiles_ref[m, b] for b in range(tiles_ref.shape[1])], axis=1)


def updates_kernel(grads_ref, warm_ref, act_ref, error_ref, high_ref, low_ref, term_ref, grads_t):
    @pl.when(pl.program_id(0) == 0)
    def _():
        for m in range(2):
            grads_t[m * LANES : (m + 1) * LANES] = grads_ref[m].T

    errors = jnp.concatenate([error_ref[m, 0].T for m in range(2)], axis=0)
    updates = dot(grads_t[...], act_ref[...]) + errors.astype(F32)
    high, low = split(updates)
    high_ref[...] = high
    low_ref[...] = low
    warm = block_diagonal([warm_ref[m].T for m in range(2)])
    store_tiles(term_ref, left_terms(warm, high, low))


def make_updates(activations, output_grads, error_feedback, warm_start):
    tokens, d = activations.shape
    block = min(1024, d)
    wide = 2 * LANES
    return pl.pallas_call(
        updates_kernel,
        grid=(d // block,),
        in_specs=[
            pl.BlockSpec(output_grads.shape, lambda i: (0, 0, 0)),
            pl.BlockSpec(warm_start.shape, lambda i: (0, 0, 0)),
            pl.BlockSpec((tokens, block), lambda i: (0, i)),
            pl.BlockSpec((2, 1, block, LANES), lambda i: (0, 0, i, 0)),
        ],
        out_specs=[
            pl.BlockSpec((wide, block), lambda i: (0, i)),
            pl.BlockSpec((wide, block), lambda i: (0, i)),
            pl.BlockSpec((2, block // LANES, RANK, LANES), lambda i: (0, i, 0, 0)),
        ],
        out_shape=[
            jax.ShapeDtypeStruct((wide, d), BF16),
            jax.ShapeDtypeStruct((wide, d), BF16),
            jax.ShapeDtypeStruct((2, d // LANES, RANK, LANES), F32),
        ],
        scratch_shapes=[pltpu.VMEM((wide, tokens), BF16)],
        compiler_params=pltpu.CompilerParams(vmem_limit_bytes=28 << 20),
        name="updates",
    )(output_grads, warm_start, activations, error_feedback)


def inverse_of_factor(gram):
    row = lax.broadcasted_iota(jnp.int32, (RANK, 2 * RANK), 0)
    column = lax.broadcasted_iota(jnp.int32, (RANK, 2 * RANK), 1)
    table = jnp.concatenate([gram, jnp.zeros_like(gram)], axis=1)
    table = jnp.where(column == row + RANK, jnp.float32(1), table)
    for k in range(RANK):
        scale = 1.0 / jnp.sqrt(table[k : k + 1, k : k + 1])
        pivot = table[k : k + 1, :] * scale
        below = table - (table[:, k : k + 1] * scale) * pivot
        table = jnp.where(row > k, below, jnp.where(row == k, pivot, table))
    return table[:, RANK:]


def right_kernel(last, tiles_ref, high_ref, low_ref, out_ref):
    sums = [rows_of(tiles_ref, m) for m in range(2)]
    both = jnp.concatenate(sums, axis=0)
    s_high, s_low = split(both)
    pair = dot(jnp.concatenate([s_high, s_low], axis=0), high_ref[...], NT)
    right = pair[:16] + pair[16:] + dot(s_high, low_ref[...], NT)
    for m in range(2):
        gram = lax.dot_general(sums[m], sums[m], NT, precision=HIGHEST, preferred_element_type=F32)
        inverse = inverse_of_factor(gram)
        mine = right[m * RANK : (m + 1) * RANK, m * LANES : (m + 1) * LANES]
        factor = lax.dot_general(inverse, mine, (((1,), (0,)), ((), ())), precision=HIGHEST, preferred_element_type=F32)
        if last:
            factor = lax.dot_general(inverse, factor, TN, precision=HIGHEST, preferred_element_type=F32)
        for copy in range(out_ref.shape[0]):
            out_ref[copy, m] = factor


def right_terms(last, copies, tiles, high, low):
    return pl.pallas_call(
        functools.partial(right_kernel, last),
        out_shape=jax.ShapeDtypeStruct((copies, 2, RANK, LANES), F32),
        compiler_params=pltpu.CompilerParams(vmem_limit_bytes=28 << 20),
        name="right",
    )(tiles, high, low)


def total_rows(parts_ref):
    return [sum(parts_ref[r, m] for r in range(parts_ref.shape[0])) for m in range(2)]


def left_kernel(parts_ref, high_ref, low_ref, term_ref):
    factor = block_diagonal(total_rows(parts_ref))
    store_tiles(term_ref, left_terms(factor, high_ref[...], low_ref[...]))


def left_call(parts, high, low):
    wide, d = high.shape
    block = min(2048, d)
    return pl.pallas_call(
        left_kernel,
        grid=(d // block,),
        in_specs=[
            pl.BlockSpec(parts.shape, lambda i: (0, 0, 0, 0)),
            pl.BlockSpec((wide, block), lambda i: (0, i)),
            pl.BlockSpec((wide, block), lambda i: (0, i)),
        ],
        out_specs=pl.BlockSpec((2, block // LANES, RANK, LANES), lambda i: (0, i, 0, 0)),
        out_shape=jax.ShapeDtypeStruct((2, d // LANES, RANK, LANES), F32),
        compiler_params=pltpu.CompilerParams(vmem_limit_bytes=28 << 20),
        name="left",
    )(parts, high, low)


def spread_kernel(parts_ref, out_ref):
    total = parts_ref[0]
    for r in range(1, parts_ref.shape[0]):
        total = total + parts_ref[r]
    for r in range(parts_ref.shape[0]):
        out_ref[r] = total


def spread_sum(parts):
    return pl.pallas_call(
        spread_kernel,
        out_shape=jax.ShapeDtypeStruct(parts.shape, F32),
        compiler_params=pltpu.CompilerParams(vmem_limit_bytes=8 << 20),
        name="spread",
    )(parts)


def sum_everywhere(tiles):
    shape = tiles.shape
    flat = tiles.reshape((shape[0] * shape[1],) + shape[2:])
    mine = lax.all_to_all(flat, EVERY, 0, 0)
    return lax.all_to_all(spread_sum(mine), EVERY, 0, 0).reshape(shape)


def mean_columns(weights, tiles):
    w_high, w_low = split(weights)
    t_high, t_low = split(tiles)
    left = jnp.concatenate([w_high, w_high, w_low], axis=0)
    right = jnp.concatenate([t_high, t_low, t_high], axis=0)
    return dot(left, right, TN)


def final_kernel(replicas, own_ref, parts_ref, all_tiles_ref, tiles_ref, high_ref, low_ref, decoded_ref, error_ref):
    weights = [w / replicas for w in total_rows(parts_ref)]

    @pl.when(pl.program_id(0) == 0)
    def _():
        own = own_ref[0]
        count = decoded_ref.shape[1] // LANES
        for m in range(2):
            tiles = jnp.concatenate([all_tiles_ref[m, own * count + b] for b in range(count)], axis=1)
            decoded_ref[m] = mean_columns(weights[m], tiles).T.astype(BF16)

    for m in range(2):
        part = pl.ds(m * LANES, LANES)
        updates = high_ref[part, :].astype(F32) + low_ref[part, :].astype(F32)
        rest = updates - mean_columns(weights[m], rows_of(tiles_ref, m))
        error_ref[m, 0] = rest.astype(BF16).T


def final_call(own, replicas, parts, tiles, high, low):
    wide, d = high.shape
    block = min(1024, d)
    return pl.pallas_call(
        functools.partial(final_kernel, replicas),
        grid_spec=pltpu.PrefetchScalarGridSpec(
            num_scalar_prefetch=1,
            grid=(d // block,),
            in_specs=[
                pl.BlockSpec(parts.shape, lambda i, own: (0, 0, 0, 0)),
                pl.BlockSpec(tiles.shape, lambda i, own: (0, 0, 0, 0)),
                pl.BlockSpec((2, block // LANES, RANK, LANES), lambda i, own: (0, i, 0, 0)),
                pl.BlockSpec((wide, block), lambda i, own: (0, i)),
                pl.BlockSpec((wide, block), lambda i, own: (0, i)),
            ],
            out_specs=[
                pl.BlockSpec((2, d // replicas, LANES), lambda i, own: (0, 0, 0)),
                pl.BlockSpec((2, 1, block, LANES), lambda i, own: (0, 0, i, 0)),
            ],
        ),
        out_shape=[
            jax.ShapeDtypeStruct((2, d // replicas, LANES), BF16),
            jax.ShapeDtypeStruct((2, 1, d, LANES), BF16),
        ],
        compiler_params=pltpu.CompilerParams(vmem_limit_bytes=28 << 20),
        name="final",
    )(own, parts, tiles, tiles, high, low)


def local(activations, output_grads, error_feedback, warm_start):
    replicas = lax.axis_size("dp")
    high, low, term = make_updates(activations, output_grads, error_feedback, warm_start)
    summed = sum_everywhere(term)
    parts = lax.all_to_all(right_terms(False, replicas, summed, high, low), "dp", 0, 0)
    summed = sum_everywhere(left_call(parts, high, low))
    parts = lax.all_to_all(right_terms(True, replicas, summed, high, low), "dp", 0, 0)
    own = lax.axis_index("dp").reshape(1)
    return tuple(final_call(own, replicas, parts, summed, high, low))


def solution(mesh):
    placed = (
        P("dp", None),
        P(None, "dp", "tensor"),
        P(None, "dp", None, "tensor"),
        P(None, "tensor", None),
    )
    return jax.shard_map(
        local,
        mesh=mesh,
        in_specs=placed,
        out_specs=(P(None, "dp", "tensor"), P(None, "dp", None, "tensor")),
        check_vma=False,
    )
```

```python
import functools

import jax
import jax.numpy as jnp
from jax import lax
from jax.experimental import pallas as pl
from jax.experimental.pallas import tpu as pltpu
from jax.sharding import PartitionSpec as P

RANK = 8
CHUNK = 1024
LANES = 128
F32, BF16 = jnp.float32, jnp.bfloat16
HIGHEST = lax.Precision.HIGHEST
EVERY = ("dp", "tensor")
NN = (((1,), (0,)), ((), ()))
NT = (((1,), (1,)), ((), ()))
TN = (((0,), (0,)), ((), ()))
WHOLE = pl.BlockSpec(memory_space=pltpu.VMEM)
in_vmem = functools.partial(pltpu.with_memory_space_constraint, memory_space=pltpu.VMEM)
in_hbm = functools.partial(pltpu.with_memory_space_constraint, memory_space=pltpu.HBM)


def params(mebibytes):
    return pltpu.CompilerParams(vmem_limit_bytes=mebibytes << 20)


def split(x):
    high = x.astype(BF16)
    return high, (x - high.astype(F32)).astype(BF16)


def dot(x, y, dims=NN):
    return lax.dot_general(x, y, dims, preferred_element_type=F32)


def exact_dot(x, y, dims=NN):
    return lax.dot_general(x, y, dims, precision=HIGHEST, preferred_element_type=F32)


def two_terms(x):
    return jnp.concatenate(split(x), axis=0)


def folded(pair):
    half = pair.shape[0] // 2
    return pair[:half] + pair[half:]


def block_diagonal(rows):
    zero = jnp.zeros_like(rows[0])
    top = jnp.concatenate([rows[0], zero], axis=1)
    bottom = jnp.concatenate([zero, rows[1]], axis=1)
    return jnp.concatenate([top, bottom], axis=0)


def store_tiles(out_ref, terms, first=0):
    for m in range(2):
        for b in range(terms.shape[1] // LANES):
            out_ref[m, first + b] = terms[m * RANK : (m + 1) * RANK, b * LANES : (b + 1) * LANES]


def rows_of(tiles_ref, m, first=0, count=None):
    count = tiles_ref.shape[1] if count is None else count
    return jnp.concatenate([tiles_ref[m, first + b] for b in range(count)], axis=1)


def updates_kernel(chunk, act_ref, grads_ref, error_ref, warm_ref, high_ref, low_ref, term_ref, act, grads, errors, sems):
    tokens, d = act.shape
    parts = [pl.ds(first, chunk) for first in range(0, d, chunk)]
    grads_copy = pltpu.make_async_copy(grads_ref, grads, sems.at[0])
    grads_copy.start()
    copies = []
    for i, part in enumerate(parts):
        copies.append(
            [
                pltpu.make_async_copy(error_ref.at[:, :, part], errors.at[:, :, part], sems.at[2 * i + 1]),
                pltpu.make_async_copy(act_ref.at[:, part], act.at[:, part], sems.at[2 * i + 2]),
            ]
        )
        for copy in copies[-1]:
            copy.start()
    warm = [two_terms(warm_ref[m]) for m in range(2)]
    identity = jnp.where(
        lax.broadcasted_iota(jnp.int32, (LANES, LANES), 0) == lax.broadcasted_iota(jnp.int32, (LANES, LANES), 1), 1.0, 0.0
    ).astype(BF16)
    turn = [jnp.concatenate([identity, warm[m]], axis=0) for m in range(2)]
    grads_copy.wait()
    taken = two_terms(jnp.concatenate([folded(dot(warm[m], grads[m], NT)) for m in range(2)], axis=0))
    weights = jnp.concatenate([grads[0].T, grads[1].T, taken], axis=0)
    wide = 2 * LANES
    for i, part in enumerate(parts):
        for copy in copies[i]:
            copy.wait()
        turned = [dot(turn[m], errors[m, 0, part], NT) for m in range(2)]
        products = dot(weights, act[:, part])
        high, low = split(products[:wide] + jnp.concatenate([t[:LANES] for t in turned], axis=0))
        high_ref[:, part] = high
        low_ref[:, part] = low
        terms = jnp.concatenate([folded(t[LANES:]) for t in turned], axis=0)
        store_tiles(term_ref, folded(products[wide:]) + terms, i * chunk // LANES)


def make_updates(activations, output_grads, error_feedback, warm_rows):
    tokens, d = activations.shape
    chunk = min(CHUNK, d)
    wide = 2 * LANES
    loaded = (activations, output_grads, error_feedback)
    return pl.pallas_call(
        functools.partial(updates_kernel, chunk),
        in_specs=[pl.BlockSpec(memory_space=pl.ANY)] * 3 + [WHOLE],
        out_specs=[WHOLE] * 3,
        out_shape=[pltpu.VMEM((wide, d), BF16)] * 2 + [jax.ShapeDtypeStruct((2, d // LANES, RANK, LANES), F32)],
        scratch_shapes=[pltpu.VMEM(x.shape, x.dtype) for x in loaded] + [pltpu.SemaphoreType.DMA((1 + 2 * (d // chunk),))],
        compiler_params=params(32),
        name="updates",
    )(*map(in_hbm, loaded), warm_rows)


def inverse_of_factor(gram):
    row = lax.broadcasted_iota(jnp.int32, (RANK, 2 * RANK), 0)
    column = lax.broadcasted_iota(jnp.int32, (RANK, 2 * RANK), 1)
    table = jnp.concatenate([gram, jnp.zeros_like(gram)], axis=1)
    table = jnp.where(column == row + RANK, jnp.float32(1), table)
    pivots = jnp.zeros((RANK, 2 * RANK), F32)
    for k in range(RANK):
        along = jnp.broadcast_to(table[:, k : k + 1], table.shape)
        pivot = jnp.broadcast_to(along[k : k + 1, :], table.shape)
        pivots = jnp.where(row == k, pivot, pivots)
        table = jnp.where(row > k, table - (along / pivot) * table[k : k + 1, :], table)
    return (table * (1.0 / jnp.sqrt(pivots)))[:, RANK:]


def right_kernel(last, tiles_ref, high_ref, low_ref, out_ref):
    sums = [rows_of(tiles_ref, m) for m in range(2)]
    grams = [exact_dot(rows, rows, NT) for rows in sums]
    s_high, s_low = split(jnp.concatenate(sums, axis=0))
    pair = dot(jnp.concatenate([s_high, s_low], axis=0), high_ref[...], NT)
    right = folded(pair) + dot(s_high, low_ref[...], NT)
    inverses = [inverse_of_factor(gram) for gram in grams]
    for m in range(2):
        norm = exact_dot(inverses[m], inverses[m], TN) if last else inverses[m]
        mine = exact_dot(norm, right[m * RANK : (m + 1) * RANK, m * LANES : (m + 1) * LANES])
        for copy in range(out_ref.shape[0]):
            out_ref[copy, m] = mine


def right_terms(last, copies, tiles, high, low):
    return pl.pallas_call(
        functools.partial(right_kernel, last),
        in_specs=[WHOLE] * 3,
        out_specs=WHOLE,
        out_shape=jax.ShapeDtypeStruct((copies, 2, RANK, LANES), F32),
        compiler_params=params(24),
        name="right",
    )(tiles, in_vmem(high), in_vmem(low))


def totals(parts_ref):
    return [sum(parts_ref[r, m] for r in range(parts_ref.shape[0])) for m in range(2)]


def left_kernel(parts_ref, high_ref, low_ref, term_ref):
    f_high, f_low = split(block_diagonal(totals(parts_ref)))
    both = jnp.concatenate([f_high, f_low], axis=0)
    step = min(2048, high_ref.shape[1])
    for first in range(0, high_ref.shape[1], step):
        part = pl.ds(first, step)
        terms = folded(dot(both, high_ref[:, part])) + dot(f_high, low_ref[:, part])
        store_tiles(term_ref, terms, first // LANES)


def left_terms(parts, high, low):
    return pl.pallas_call(
        left_kernel,
        in_specs=[WHOLE] * 3,
        out_specs=WHOLE,
        out_shape=jax.ShapeDtypeStruct((2, high.shape[1] // LANES, RANK, LANES), F32),
        compiler_params=params(24),
        name="left",
    )(parts, in_vmem(high), in_vmem(low))


def spread_kernel(parts_ref, out_ref):
    total = parts_ref[0]
    for r in range(1, parts_ref.shape[0]):
        total = total + parts_ref[r]
    for r in range(parts_ref.shape[0]):
        out_ref[r] = total


def spread_sum(parts):
    return pl.pallas_call(
        spread_kernel,
        in_specs=[WHOLE],
        out_specs=WHOLE,
        out_shape=jax.ShapeDtypeStruct(parts.shape, F32),
        compiler_params=params(8),
        name="spread",
    )(parts)


def scatter_sum(tiles):
    return lax.all_to_all(tiles.reshape((-1,) + tiles.shape[2:]), EVERY, 0, 0)


def gather_sum(parts, shape):
    return lax.all_to_all(spread_sum(parts), EVERY, 0, 0).reshape(shape)


def mean_columns(weights, tiles):
    w_high, w_low = split(weights)
    t_high, t_low = split(tiles)
    left = jnp.concatenate([w_high, w_high, w_low], axis=0)
    right = jnp.concatenate([t_high, t_low, t_high], axis=0)
    return dot(left, right, TN)


def final_kernel(replicas, block, parts_ref, tiles_ref, high_ref, low_ref, decoded_ref, error_ref, held, sems):
    weights = [w / replicas for w in totals(parts_ref)]
    copies = []
    for i in range(high_ref.shape[1] // block):
        columns = pl.ds(i * block, block)
        for m in range(2):
            part = pl.ds(m * LANES, LANES)
            updates = high_ref[part, columns].astype(F32) + low_ref[part, columns].astype(F32)
            tiles = rows_of(tiles_ref, m, i * block // LANES, block // LANES)
            held[m, 0, columns] = (updates - mean_columns(weights[m], tiles)).astype(BF16).T
        copy = pltpu.make_async_copy(held.at[:, :, columns], error_ref.at[:, :, columns], sems.at[i])
        copy.start()
        copies.append(copy)
    count = decoded_ref.shape[1] // LANES
    for m in range(2):
        tiles = rows_of(tiles_ref, m, lax.axis_index("dp") * count, count)
        decoded_ref[m] = mean_columns(weights[m], tiles).T.astype(BF16)
    for copy in copies:
        copy.wait()


def final_outputs(replicas, parts, tiles, high, low):
    d = high.shape[1]
    block = min(1024, d)
    return pl.pallas_call(
        functools.partial(final_kernel, replicas, block),
        in_specs=[WHOLE] * 4,
        out_specs=[WHOLE, pl.BlockSpec(memory_space=pl.ANY)],
        out_shape=[
            jax.ShapeDtypeStruct((2, d // replicas, LANES), BF16),
            jax.ShapeDtypeStruct((2, 1, d, LANES), BF16),
        ],
        scratch_shapes=[pltpu.VMEM((2, 1, d, LANES), BF16), pltpu.SemaphoreType.DMA((d // block,))],
        compiler_params=params(24),
        name="final",
    )(parts, tiles, in_vmem(high), in_vmem(low))


def local(activations, output_grads, error_feedback, warm_start):
    replicas = lax.axis_size("dp")
    high, low, term = make_updates(activations, output_grads, error_feedback, jnp.swapaxes(warm_start, 1, 2))
    summed = gather_sum(scatter_sum(term), term.shape)
    parts = lax.all_to_all(right_terms(False, replicas, summed, high, low), "dp", 0, 0)
    summed = gather_sum(scatter_sum(left_terms(parts, high, low)), term.shape)
    parts = lax.all_to_all(right_terms(True, replicas, summed, high, low), "dp", 0, 0)
    return tuple(final_outputs(replicas, parts, summed, high, low))


def solution(mesh):
    placed = (
        P("dp", None),
        P(None, "dp", "tensor"),
        P(None, "dp", None, "tensor"),
        P(None, "tensor", None),
    )
    return jax.shard_map(
        local,
        mesh=mesh,
        in_specs=placed,
        out_specs=(P(None, "dp", "tensor"), P(None, "dp", None, "tensor")),
        check_vma=False,
    )
```

```python
import functools

import jax
import jax.numpy as jnp
from jax import lax
from jax.experimental import pallas as pl
from jax.experimental.pallas import tpu as pltpu
from jax.sharding import Mesh, PartitionSpec as P

RANK = 8
CHUNK = 1024
LANES = 128
F32, BF16 = jnp.float32, jnp.bfloat16
HIGHEST = lax.Precision.HIGHEST
NN = (((1,), (0,)), ((), ()))
NT = (((1,), (1,)), ((), ()))
TN = (((0,), (0,)), ((), ()))
WHOLE = pl.BlockSpec(memory_space=pltpu.VMEM)
in_vmem = functools.partial(pltpu.with_memory_space_constraint, memory_space=pltpu.VMEM)
in_hbm = functools.partial(pltpu.with_memory_space_constraint, memory_space=pltpu.HBM)


def params(mebibytes):
    return pltpu.CompilerParams(vmem_limit_bytes=mebibytes << 20)


def split(x):
    high = x.astype(BF16)
    return high, (x - high.astype(F32)).astype(BF16)


def dot(x, y, dims=NN):
    return lax.dot_general(x, y, dims, preferred_element_type=F32)


def exact_dot(x, y, dims=NN):
    return lax.dot_general(x, y, dims, precision=HIGHEST, preferred_element_type=F32)


def two_terms(x):
    return jnp.concatenate(split(x), axis=0)


def folded(pair):
    half = pair.shape[0] // 2
    return pair[:half] + pair[half:]


def store_tiles(out_ref, terms, first=0):
    for b in range(terms.shape[1] // LANES):
        for m in range(2):
            out_ref[first + b, m] = terms[m * RANK : (m + 1) * RANK, b * LANES : (b + 1) * LANES]


def rows_of(tiles_ref, first=0, count=None):
    count = tiles_ref.shape[0] if count is None else count
    return jnp.concatenate([tiles_ref[first + b] for b in range(count)], axis=1)


def own_matrix():
    return lax.axis_index("core")


def rows_at(m):
    return pl.ds(pl.multiple_of(m * LANES, LANES), LANES)


def updates_kernel(chunk, act_ref, grads_ref, error_ref, rows_ref, high_ref, low_ref, term_ref, act, grads, errors, rows, sems):
    tokens, d = act.shape
    parts = [pl.ds(first, chunk) for first in range(0, d, chunk)]
    grads_copy = pltpu.make_async_copy(grads_ref, grads, sems.at[0])
    rows_copy = pltpu.make_async_copy(rows_ref, rows, sems.at[2 * len(parts) + 1])
    rows_copy.start()
    grads_copy.start()
    copies = []
    for i, part in enumerate(parts):
        copies.append(
            [
                pltpu.make_async_copy(error_ref.at[:, :, part], errors.at[:, :, part], sems.at[2 * i + 1]),
                pltpu.make_async_copy(act_ref.at[:, part], act.at[:, part], sems.at[2 * i + 2]),
            ]
        )
        for copy in copies[-1]:
            copy.start()
    rows_copy.wait()
    warm = [two_terms(rows[m]) for m in range(2)]
    identity = jnp.where(
        lax.broadcasted_iota(jnp.int32, (LANES, LANES), 0) == lax.broadcasted_iota(jnp.int32, (LANES, LANES), 1), 1.0, 0.0
    ).astype(BF16)
    turn = [jnp.concatenate([identity, warm[m]], axis=0) for m in range(2)]
    grads_copy.wait()
    taken = two_terms(jnp.concatenate([folded(dot(warm[m], grads[m], NT)) for m in range(2)], axis=0))
    weights = jnp.concatenate([grads[0].T, grads[1].T, taken], axis=0)
    wide = 2 * LANES
    for i, part in enumerate(parts):
        for copy in copies[i]:
            copy.wait()
        turned = [dot(turn[m], errors[m, 0, part], NT) for m in range(2)]
        products = dot(weights, act[:, part])
        high, low = split(products[:wide] + jnp.concatenate([t[:LANES] for t in turned], axis=0))
        high_ref[:, part] = high
        low_ref[:, part] = low
        terms = jnp.concatenate([folded(t[LANES:]) for t in turned], axis=0)
        store_tiles(term_ref, folded(products[wide:]) + terms, i * chunk // LANES)


def make_updates(activations, output_grads, error_feedback, warm_rows):
    tokens, d = activations.shape
    chunk = min(CHUNK, d)
    wide = 2 * LANES
    loaded = (activations, output_grads, error_feedback, warm_rows)
    return pl.pallas_call(
        functools.partial(updates_kernel, chunk),
        in_specs=[pl.BlockSpec(memory_space=pl.ANY)] * 4,
        out_specs=[WHOLE] * 3,
        out_shape=[pltpu.VMEM((wide, d), BF16)] * 2 + [jax.ShapeDtypeStruct((d // LANES, 2, RANK, LANES), F32)],
        scratch_shapes=[pltpu.VMEM(x.shape, x.dtype) for x in loaded] + [pltpu.SemaphoreType.DMA((2 + 2 * (d // chunk),))],
        compiler_params=params(32),
        name="updates",
    )(*map(in_hbm, loaded))


def inverse_of_factor(gram):
    row = lax.broadcasted_iota(jnp.int32, (RANK, 2 * RANK), 0)
    column = lax.broadcasted_iota(jnp.int32, (RANK, 2 * RANK), 1)
    table = jnp.concatenate([gram, jnp.zeros_like(gram)], axis=1)
    table = jnp.where(column == row + RANK, jnp.float32(1), table)
    pivots = jnp.zeros((RANK, 2 * RANK), F32)
    for k in range(RANK):
        along = jnp.broadcast_to(table[:, k : k + 1], table.shape)
        pivot = jnp.broadcast_to(along[k : k + 1, :], table.shape)
        pivots = jnp.where(row == k, pivot, pivots)
        table = jnp.where(row > k, table - (along / pivot) * table[k : k + 1, :], table)
    return (table * (1.0 / jnp.sqrt(pivots)))[:, RANK:]


def right_rows(last, m, tiles_ref, high_ref, low_ref):
    rows = rows_of(tiles_ref)
    first, second = split(rows)
    third = (rows - first.astype(F32) - second.astype(F32)).astype(BF16)
    three = jnp.concatenate([first, second, third], axis=0)
    gram = dot(three, three, NT)
    gram = sum(gram[i * RANK : (i + 1) * RANK] for i in range(3))
    gram = sum(gram[:, i * RANK : (i + 1) * RANK] for i in range(3))
    part = rows_at(m)
    right = folded(dot(three[: 2 * RANK], high_ref[part, :], NT)) + dot(first, low_ref[part, :], NT)
    inverse = inverse_of_factor(gram)
    if last:
        inverse = exact_dot(inverse, inverse, TN)
    return exact_dot(inverse, right)


def right_own_kernel(last, tiles_ref, high_ref, low_ref, out_ref):
    out_ref[...] = right_rows(last, own_matrix(), tiles_ref, high_ref, low_ref)


def right_both_kernel(last, mine_ref, tiles_ref, high_ref, low_ref, out_ref):
    own = own_matrix()
    mine = mine_ref[...]
    other = right_rows(last, 1 - own, tiles_ref, high_ref, low_ref)
    for copy in range(out_ref.shape[0]):
        out_ref[copy, own] = mine
        out_ref[copy, 1 - own] = other


def right_terms(last, copies, tiles, high, low):
    other = lax.ppermute(tiles, "core", [(0, 1), (1, 0)])
    shared = dict(out_specs=WHOLE, compiler_params=params(24))
    mine = pl.pallas_call(
        functools.partial(right_own_kernel, last),
        in_specs=[WHOLE] * 3,
        out_shape=jax.ShapeDtypeStruct((RANK, LANES), F32),
        name="right_own",
        **shared,
    )(tiles, in_vmem(high), in_vmem(low))
    both = pl.pallas_call(
        functools.partial(right_both_kernel, last),
        in_specs=[WHOLE] * 4,
        out_shape=jax.ShapeDtypeStruct((copies, 2, RANK, LANES), F32),
        name="right_both",
        **shared,
    )(mine, other, in_vmem(high), in_vmem(low))
    return both, other


def total(parts_ref, m):
    return sum(parts_ref[r, m] for r in range(parts_ref.shape[0]))


def left_kernel(mine, parts_ref, high_ref, low_ref, term_ref):
    m = own_matrix() if mine else 1 - own_matrix()
    part = rows_at(m)
    f_high, f_low = split(total(parts_ref, m))
    both = jnp.concatenate([f_high, f_low], axis=0)
    step = min(2048, high_ref.shape[1])
    for first in range(0, high_ref.shape[1], step):
        columns = pl.ds(first, step)
        terms = folded(dot(both, high_ref[part, columns])) + dot(f_high, low_ref[part, columns])
        for b in range(step // LANES):
            term_ref[first // LANES + b] = terms[:, b * LANES : (b + 1) * LANES]


def left_terms(mine, parts, high, low):
    return pl.pallas_call(
        functools.partial(left_kernel, mine),
        in_specs=[WHOLE] * 3,
        out_specs=WHOLE,
        out_shape=jax.ShapeDtypeStruct((high.shape[1] // LANES, RANK, LANES), F32),
        compiler_params=params(24),
        name="left_own" if mine else "left_other",
    )(parts, in_vmem(high), in_vmem(low))


def add_kernel(x_ref, y_ref, out_ref):
    out_ref[...] = x_ref[...] + y_ref[...]


def chip_terms(parts, high, low):
    sent = lax.ppermute(left_terms(False, parts, high, low), "core", [(0, 1), (1, 0)])
    kept = left_terms(True, parts, high, low)
    return pl.pallas_call(
        add_kernel,
        in_specs=[WHOLE] * 2,
        out_specs=WHOLE,
        out_shape=jax.ShapeDtypeStruct(kept.shape, F32),
        compiler_params=params(8),
        name="add",
    )(sent, kept)


def spread_kernel(parts_ref, out_ref):
    total = parts_ref[0]
    for r in range(1, parts_ref.shape[0]):
        total = total + parts_ref[r]
    for r in range(out_ref.shape[0]):
        out_ref[r] = total


def spread_sum(parts, copies):
    return pl.pallas_call(
        spread_kernel,
        in_specs=[WHOLE],
        out_specs=WHOLE,
        out_shape=jax.ShapeDtypeStruct((copies,) + parts.shape[1:], F32),
        compiler_params=params(8),
        name="spread",
    )(parts)


def sum_own(tiles, axes):
    copies = tiles.shape[0]
    parts = lax.all_to_all(tiles.reshape((-1,) + tiles.shape[-2:]), axes, 0, 0)
    return lax.all_to_all(spread_sum(parts, copies), ("dp", "x"), 0, 0)


def mean_columns(weights, tiles):
    w_high, w_low = split(weights)
    t_high, t_low = split(tiles)
    left = jnp.concatenate([w_high, w_high, w_low], axis=0)
    right = jnp.concatenate([t_high, t_low, t_high], axis=0)
    return dot(left, right, TN)


def final_kernel(replicas, block, parts_ref, mine_ref, other_ref, high_ref, low_ref, decoded_ref, error_ref, held, sems):
    weights = [total(parts_ref, m) / replicas for m in range(2)]
    own = own_matrix()

    def mean(m, first, count):
        mine, other = (rows_of(ref, first, count) for ref in (mine_ref, other_ref))
        return mean_columns(weights[m], jnp.where(own == m, mine, other))

    copies = []
    for i in range(high_ref.shape[1] // block):
        columns = pl.ds(i * block, block)
        for m in range(2):
            part = pl.ds(m * LANES, LANES)
            updates = high_ref[part, columns].astype(F32) + low_ref[part, columns].astype(F32)
            held[m, 0, columns] = (updates - mean(m, i * block // LANES, block // LANES)).astype(BF16).T
        copy = pltpu.make_async_copy(held.at[:, :, columns], error_ref.at[:, :, columns], sems.at[i])
        copy.start()
        copies.append(copy)
    count = decoded_ref.shape[1] // LANES
    for m in range(2):
        decoded_ref[m] = mean(m, lax.axis_index("dp") * count, count).T.astype(BF16)
    for copy in copies:
        copy.wait()


def final_outputs(replicas, parts, mine, other, high, low):
    d = high.shape[1]
    block = min(1024, d)
    return pl.pallas_call(
        functools.partial(final_kernel, replicas, block),
        in_specs=[WHOLE] * 5,
        out_specs=[WHOLE, pl.BlockSpec(memory_space=pl.ANY)],
        out_shape=[
            jax.ShapeDtypeStruct((2, d // replicas, LANES), BF16),
            jax.ShapeDtypeStruct((2, 1, d, LANES), BF16),
        ],
        scratch_shapes=[
            pltpu.VMEM((2, 1, d, LANES), BF16),
            pltpu.SemaphoreType.DMA((d // block,)),
        ],
        compiler_params=params(24),
        name="final",
    )(parts, mine, other, in_vmem(high), in_vmem(low))


def local(activations, output_grads, error_feedback, warm_start):
    replicas = lax.axis_size("dp")
    high, low, term = make_updates(activations, output_grads, error_feedback, jnp.swapaxes(warm_start, 1, 2))
    mine = sum_own(term, ("dp", "x", "core"))
    terms, other = right_terms(False, replicas, mine, high, low)
    parts = lax.all_to_all(terms, "dp", 0, 0)
    mine = sum_own(chip_terms(parts, high, low), ("dp", "x"))
    terms, other = right_terms(True, replicas, mine, high, low)
    parts = lax.all_to_all(terms, "dp", 0, 0)
    return tuple(final_outputs(replicas, parts, mine, other, high, low))


def solution(mesh):
    replicas, width = mesh.devices.shape
    split_mesh = Mesh(mesh.devices.reshape(replicas, width // 2, 2), ("dp", "x", "core"))
    tensor = ("x", "core")
    return jax.shard_map(
        local,
        mesh=split_mesh,
        in_specs=(P("dp", None), P(None, "dp", tensor), P(None, "dp", None, tensor), P(None, tensor, None)),
        out_specs=(P(None, "dp", tensor), P(None, "dp", None, tensor)),
        check_vma=False,
    )
```

```python
import functools

import jax
import jax.numpy as jnp
from jax import lax
from jax.experimental import pallas as pl
from jax.experimental.pallas import tpu as pltpu
from jax.sharding import Mesh, PartitionSpec as P

RANK = 8
CHUNK = 1024
STEP = 256
LANES = 128
F32, BF16 = jnp.float32, jnp.bfloat16
HIGHEST = lax.Precision.HIGHEST
NN = (((1,), (0,)), ((), ()))
NT = (((1,), (1,)), ((), ()))
TN = (((0,), (0,)), ((), ()))
WHOLE = pl.BlockSpec(memory_space=pltpu.VMEM)
in_vmem = functools.partial(pltpu.with_memory_space_constraint, memory_space=pltpu.VMEM)
in_hbm = functools.partial(pltpu.with_memory_space_constraint, memory_space=pltpu.HBM)


def params(mebibytes):
    return pltpu.CompilerParams(vmem_limit_bytes=mebibytes << 20)


def split(x):
    high = x.astype(BF16)
    return high, (x - high.astype(F32)).astype(BF16)


def dot(x, y, dims=NN):
    return lax.dot_general(x, y, dims, preferred_element_type=F32)


def exact_dot(x, y, dims=NN):
    return lax.dot_general(x, y, dims, precision=HIGHEST, preferred_element_type=F32)


def two_terms(x):
    return jnp.concatenate(split(x), axis=0)


def folded(pair):
    half = pair.shape[0] // 2
    return pair[:half] + pair[half:]


def rows_of(tiles_ref, first=0, count=None):
    count = tiles_ref.shape[0] if count is None else count
    return jnp.concatenate([tiles_ref[first + b] for b in range(count)], axis=1)


def own_matrix():
    return lax.axis_index("core")


def rows_at(m):
    return pl.ds(pl.multiple_of(m * LANES, LANES), LANES)


def transposed_updates(weights, act, errors):
    products = dot(weights, act)
    turned = [e.T for e in errors]
    wide = 2 * LANES
    return split(products[:wide] + jnp.concatenate(turned, axis=0).astype(F32)), products[wide:], turned


def updates_kernel(chunk, head, act_ref, grads_ref, error_ref, rows_ref, high_ref, low_ref, send_ref, keep_ref, tail_act, tail_errors, grads_t, act, grads, errors, rows, sems):
    d = high_ref.shape[1]
    rows_copy = pltpu.make_async_copy(rows_ref, rows, sems.at[0])
    grads_copy = pltpu.make_async_copy(grads_ref, grads, sems.at[1])
    rows_copy.start()
    grads_copy.start()
    places, copies = [], []
    for i in range(d // chunk):
        part = pl.ds(i * chunk, chunk)
        here = part if i < head else pl.ds((i - head) * chunk, chunk)
        act_at, error_at = (act, errors) if i < head else (tail_act, tail_errors)
        pair = [
            pltpu.make_async_copy(error_ref.at[:, :, part], error_at.at[:, :, here], sems.at[2 * i + 2]),
            pltpu.make_async_copy(act_ref.at[:, part], act_at.at[:, here], sems.at[2 * i + 3]),
        ]
        for copy in pair:
            copy.start()
        copies.append(pair)
        places.append((act_at, error_at, 0 if i < head else head * chunk))
    rows_copy.wait()
    warm = [two_terms(rows[m]) for m in range(2)]
    grads_copy.wait()
    taken = two_terms(jnp.concatenate([folded(dot(warm[m], grads[m], NT)) for m in range(2)], axis=0))
    wide = 2 * LANES
    for m in range(2):
        grads_t[m * LANES : (m + 1) * LANES] = grads[m].T
    weights = jnp.concatenate([grads_t[...], taken], axis=0)
    first_core = own_matrix() == 0
    step = min(STEP, chunk)
    for i, pair in enumerate(copies):
        act_at, error_at, shift = places[i]
        for copy in pair:
            copy.wait()
        for first in range(i * chunk, (i + 1) * chunk, step):
            here = pl.ds(first - shift, step)
            if i < head:
                part = pl.ds(first, step)
                (high, low), left, turned = transposed_updates(weights, act_at[:, here], [error_at[m, 0, here] for m in range(2)])
                high_ref[:, part] = high
                low_ref[:, part] = low
                moved = [dot(warm[m], turned[m]) for m in range(2)]
            else:
                left = dot(taken, act_at[:, here])
                moved = [dot(warm[m], error_at[m, 0, here], NT) for m in range(2)]
            terms = folded(left) + jnp.concatenate([folded(x) for x in moved], axis=0)
            key, value = terms[:RANK], terms[RANK:]
            keep, send = jnp.where(first_core, key, value), jnp.where(first_core, value, key)
            for b in range(step // LANES):
                keep_ref[first // LANES + b] = keep[:, b * LANES : (b + 1) * LANES]
                send_ref[first // LANES + b] = send[:, b * LANES : (b + 1) * LANES]


def tail_kernel(act_ref, error_ref, grads_t, keep_in, high_in, low_in, high_ref, low_ref, keep_ref):
    keep_ref[...] = keep_in[...]
    count = act_ref.shape[1]
    step = min(STEP, count)
    for first in range(0, count, step):
        here = pl.ds(first, step)
        part = pl.ds(high_ref.shape[1] - count + first, step)
        (high, low), _, _ = transposed_updates(grads_t[...], act_ref[:, here], [error_ref[m, 0, here] for m in range(2)])
        high_ref[:, part] = high
        low_ref[:, part] = low


def make_updates(activations, output_grads, error_feedback, warm_rows):
    tokens, d = activations.shape
    chunk = min(CHUNK, d)
    count = d // chunk
    head = max(1, 3 * count // 4)
    wide, early, late = 2 * LANES, head * chunk, (count - head) * chunk
    loaded = (activations, output_grads, error_feedback, warm_rows)
    tiles = jax.ShapeDtypeStruct((d // LANES, RANK, LANES), F32)
    whole = [pltpu.VMEM((wide, d), BF16)] * 2
    high, low, send, keep, act, errors, grads_t = pl.pallas_call(
        functools.partial(updates_kernel, chunk, head),
        in_specs=[pl.BlockSpec(memory_space=pl.ANY)] * 4,
        out_specs=[WHOLE] * 7,
        out_shape=whole
        + [tiles, tiles, pltpu.VMEM((tokens, late), BF16), pltpu.VMEM((2, 1, late, LANES), BF16), pltpu.VMEM((wide, tokens), BF16)],
        scratch_shapes=[
            pltpu.VMEM((tokens, early), BF16),
            pltpu.VMEM(output_grads.shape, BF16),
            pltpu.VMEM((2, 1, early, LANES), BF16),
            pltpu.VMEM(warm_rows.shape, F32),
            pltpu.SemaphoreType.DMA((2 + 2 * count,)),
        ],
        compiler_params=params(24),
        name="updates",
    )(*map(in_hbm, loaded))
    sent = lax.ppermute(send, "core", [(0, 1), (1, 0)])
    high, low, keep = pl.pallas_call(
        tail_kernel,
        in_specs=[WHOLE] * 6,
        out_specs=[WHOLE] * 3,
        out_shape=whole + [tiles],
        input_output_aliases={4: 0, 5: 1},
        compiler_params=params(8),
        name="updates_tail",
    )(*map(in_vmem, (act, errors, grads_t)), keep, in_vmem(high), in_vmem(low))
    return high, low, added(sent, keep)


def inverse_of_factor(gram):
    row = lax.broadcasted_iota(jnp.int32, (RANK, 2 * RANK), 0)
    column = lax.broadcasted_iota(jnp.int32, (RANK, 2 * RANK), 1)
    table = jnp.concatenate([gram, jnp.zeros_like(gram)], axis=1)
    table = jnp.where(column == row + RANK, jnp.float32(1), table)
    pivots = jnp.zeros((RANK, 2 * RANK), F32)
    for k in range(RANK):
        along = jnp.broadcast_to(table[:, k : k + 1], table.shape)
        pivot = jnp.broadcast_to(along[k : k + 1, :], table.shape)
        pivots = jnp.where(row == k, pivot, pivots)
        table = jnp.where(row > k, table - (along / pivot) * table[k : k + 1, :], table)
    return (table * (1.0 / jnp.sqrt(pivots)))[:, RANK:]


def right_rows(last, m, tiles_ref, high_ref, low_ref):
    rows = rows_of(tiles_ref)
    first, second = split(rows)
    third = (rows - first.astype(F32) - second.astype(F32)).astype(BF16)
    three = jnp.concatenate([first, second, third], axis=0)
    gram = dot(three, three, NT)
    gram = sum(gram[i * RANK : (i + 1) * RANK] for i in range(3))
    gram = sum(gram[:, i * RANK : (i + 1) * RANK] for i in range(3))
    part = rows_at(m)
    right = folded(dot(three[: 2 * RANK], high_ref[part, :], NT)) + dot(first, low_ref[part, :], NT)
    inverse = inverse_of_factor(gram)
    if last:
        inverse = exact_dot(inverse, inverse, TN)
    return exact_dot(inverse, right)


def right_own_kernel(last, tiles_ref, high_ref, low_ref, out_ref):
    out_ref[...] = right_rows(last, own_matrix(), tiles_ref, high_ref, low_ref)


def right_both_kernel(last, mine_ref, tiles_ref, high_ref, low_ref, out_ref):
    own = own_matrix()
    mine = mine_ref[...]
    other = right_rows(last, 1 - own, tiles_ref, high_ref, low_ref)
    for copy in range(out_ref.shape[0]):
        out_ref[copy, own] = mine
        out_ref[copy, 1 - own] = other


def right_terms(last, copies, tiles, high, low):
    other = lax.ppermute(tiles, "core", [(0, 1), (1, 0)])
    shared = dict(out_specs=WHOLE, compiler_params=params(24))
    mine = pl.pallas_call(
        functools.partial(right_own_kernel, last),
        in_specs=[WHOLE] * 3,
        out_shape=jax.ShapeDtypeStruct((RANK, LANES), F32),
        name="right_own",
        **shared,
    )(tiles, in_vmem(high), in_vmem(low))
    both = pl.pallas_call(
        functools.partial(right_both_kernel, last),
        in_specs=[WHOLE] * 4,
        out_shape=jax.ShapeDtypeStruct((copies, 2, RANK, LANES), F32),
        name="right_both",
        **shared,
    )(mine, other, in_vmem(high), in_vmem(low))
    return both, other


def total(parts_ref, m):
    return sum(parts_ref[r, m] for r in range(parts_ref.shape[0]))


def left_kernel(mine, parts_ref, high_ref, low_ref, term_ref):
    m = own_matrix() if mine else 1 - own_matrix()
    part = rows_at(m)
    f_high, f_low = split(total(parts_ref, m))
    both = jnp.concatenate([f_high, f_low], axis=0)
    step = min(2048, high_ref.shape[1])
    for first in range(0, high_ref.shape[1], step):
        columns = pl.ds(first, step)
        terms = folded(dot(both, high_ref[part, columns])) + dot(f_high, low_ref[part, columns])
        for b in range(step // LANES):
            term_ref[first // LANES + b] = terms[:, b * LANES : (b + 1) * LANES]


def left_terms(mine, parts, high, low):
    return pl.pallas_call(
        functools.partial(left_kernel, mine),
        in_specs=[WHOLE] * 3,
        out_specs=WHOLE,
        out_shape=jax.ShapeDtypeStruct((high.shape[1] // LANES, RANK, LANES), F32),
        compiler_params=params(24),
        name="left_own" if mine else "left_other",
    )(parts, in_vmem(high), in_vmem(low))


def add_kernel(x_ref, y_ref, out_ref):
    out_ref[...] = x_ref[...] + y_ref[...]


def added(x, y):
    return pl.pallas_call(
        add_kernel,
        in_specs=[WHOLE] * 2,
        out_specs=WHOLE,
        out_shape=jax.ShapeDtypeStruct(x.shape, F32),
        compiler_params=params(8),
        name="add",
    )(x, y)


def chip_terms(parts, high, low):
    sent = lax.ppermute(left_terms(False, parts, high, low), "core", [(0, 1), (1, 0)])
    return added(sent, left_terms(True, parts, high, low))


def spread_kernel(parts_ref, out_ref):
    total = parts_ref[0]
    for r in range(1, parts_ref.shape[0]):
        total = total + parts_ref[r]
    for r in range(out_ref.shape[0]):
        out_ref[r] = total


def spread_sum(parts, copies):
    return pl.pallas_call(
        spread_kernel,
        in_specs=[WHOLE],
        out_specs=WHOLE,
        out_shape=jax.ShapeDtypeStruct((copies,) + parts.shape[1:], F32),
        compiler_params=params(8),
        name="spread",
    )(parts)


def sum_own(tiles):
    parts = lax.all_to_all(tiles, ("dp", "x"), 0, 0)
    return lax.all_to_all(spread_sum(parts, tiles.shape[0]), ("dp", "x"), 0, 0)


def mean_columns(weights, tiles):
    w_high, w_low = split(weights)
    t_high, t_low = split(tiles)
    left = jnp.concatenate([w_high, w_high, w_low], axis=0)
    right = jnp.concatenate([t_high, t_low, t_high], axis=0)
    return dot(left, right, TN)


def final_kernel(replicas, block, parts_ref, mine_ref, other_ref, high_ref, low_ref, decoded_ref, error_ref, held, sems):
    weights = [total(parts_ref, m) / replicas for m in range(2)]
    own = own_matrix()

    def mean(m, first, count):
        mine, other = (rows_of(ref, first, count) for ref in (mine_ref, other_ref))
        return mean_columns(weights[m], jnp.where(own == m, mine, other))

    copies = []
    for i in range(high_ref.shape[1] // block):
        columns = pl.ds(i * block, block)
        for m in range(2):
            part = pl.ds(m * LANES, LANES)
            updates = high_ref[part, columns].astype(F32) + low_ref[part, columns].astype(F32)
            held[m, 0, columns] = (updates - mean(m, i * block // LANES, block // LANES)).astype(BF16).T
        copy = pltpu.make_async_copy(held.at[:, :, columns], error_ref.at[:, :, columns], sems.at[i])
        copy.start()
        copies.append(copy)
    count = decoded_ref.shape[1] // LANES
    for m in range(2):
        decoded_ref[m] = mean(m, lax.axis_index("dp") * count, count).T.astype(BF16)
    for copy in copies:
        copy.wait()


def final_outputs(replicas, parts, mine, other, high, low):
    d = high.shape[1]
    block = min(1024, d)
    return pl.pallas_call(
        functools.partial(final_kernel, replicas, block),
        in_specs=[WHOLE] * 5,
        out_specs=[WHOLE, pl.BlockSpec(memory_space=pl.ANY)],
        out_shape=[
            jax.ShapeDtypeStruct((2, d // replicas, LANES), BF16),
            jax.ShapeDtypeStruct((2, 1, d, LANES), BF16),
        ],
        scratch_shapes=[
            pltpu.VMEM((2, 1, d, LANES), BF16),
            pltpu.SemaphoreType.DMA((d // block,)),
        ],
        compiler_params=params(24),
        name="final",
    )(parts, mine, other, in_vmem(high), in_vmem(low))


def local(activations, output_grads, error_feedback, warm_start):
    replicas = lax.axis_size("dp")
    high, low, term = make_updates(activations, output_grads, error_feedback, jnp.swapaxes(warm_start, 1, 2))
    mine = sum_own(term)
    terms, other = right_terms(False, replicas, mine, high, low)
    parts = lax.all_to_all(terms, "dp", 0, 0)
    mine = sum_own(chip_terms(parts, high, low))
    terms, other = right_terms(True, replicas, mine, high, low)
    parts = lax.all_to_all(terms, "dp", 0, 0)
    return tuple(final_outputs(replicas, parts, mine, other, high, low))


def solution(mesh):
    replicas, width = mesh.devices.shape
    split_mesh = Mesh(mesh.devices.reshape(replicas, width // 2, 2), ("dp", "x", "core"))
    tensor = ("x", "core")
    return jax.shard_map(
        local,
        mesh=split_mesh,
        in_specs=(P("dp", None), P(None, "dp", tensor), P(None, "dp", None, tensor), P(None, tensor, None)),
        out_specs=(P(None, "dp", tensor), P(None, "dp", None, tensor)),
        check_vma=False,
    )
```

```python
import functools

import jax
import jax.numpy as jnp
from jax import lax
from jax.experimental import pallas as pl
from jax.experimental.pallas import tpu as pltpu
from jax.sharding import Mesh, PartitionSpec as P

RANK = 8
CHUNK = 1024
STEP = 256
LANES = 128
F32, BF16 = jnp.float32, jnp.bfloat16
HIGHEST = lax.Precision.HIGHEST
NN = (((1,), (0,)), ((), ()))
NT = (((1,), (1,)), ((), ()))
TN = (((0,), (0,)), ((), ()))
WHOLE = pl.BlockSpec(memory_space=pltpu.VMEM)
in_vmem = functools.partial(pltpu.with_memory_space_constraint, memory_space=pltpu.VMEM)
in_hbm = functools.partial(pltpu.with_memory_space_constraint, memory_space=pltpu.HBM)


def params(mebibytes):
    return pltpu.CompilerParams(vmem_limit_bytes=mebibytes << 20)


def split(x):
    high = x.astype(BF16)
    return high, (x - high.astype(F32)).astype(BF16)


def dot(x, y, dims=NN):
    return lax.dot_general(x, y, dims, preferred_element_type=F32)


def exact_dot(x, y, dims=NN):
    return lax.dot_general(x, y, dims, precision=HIGHEST, preferred_element_type=F32)


def two_terms(x):
    return jnp.concatenate(split(x), axis=0)


def folded(pair):
    half = pair.shape[0] // 2
    return pair[:half] + pair[half:]


def rows_of(tiles_ref, first=0, count=None):
    count = tiles_ref.shape[0] if count is None else count
    return jnp.concatenate([tiles_ref[first + b] for b in range(count)], axis=1)


def own_matrix():
    return lax.axis_index("core")


def swapped(x):
    return lax.ppermute(x, "core", [(0, 1), (1, 0)])


def rows_at(m):
    return pl.ds(pl.multiple_of(m * LANES, LANES), LANES)


def transposed_updates(weights, act, errors):
    products = dot(weights, act)
    turned = [e.T for e in errors]
    wide = 2 * LANES
    return split(products[:wide] + jnp.concatenate(turned, axis=0).astype(F32)), products[wide:], turned


def updates_kernel(chunk, head, act_ref, grads_ref, error_ref, rows_ref, high_ref, low_ref, send_ref, keep_ref, tail_act, tail_errors, grads_t, act, grads, errors, rows, sems):
    d = high_ref.shape[1]
    rows_copy = pltpu.make_async_copy(rows_ref, rows, sems.at[0])
    grads_copy = pltpu.make_async_copy(grads_ref, grads, sems.at[1])
    rows_copy.start()
    grads_copy.start()
    places, copies = [], []
    for i in range(d // chunk):
        part = pl.ds(i * chunk, chunk)
        here = part if i < head else pl.ds((i - head) * chunk, chunk)
        act_at, error_at = (act, errors) if i < head else (tail_act, tail_errors)
        pair = [
            pltpu.make_async_copy(error_ref.at[:, :, part], error_at.at[:, :, here], sems.at[2 * i + 2]),
            pltpu.make_async_copy(act_ref.at[:, part], act_at.at[:, here], sems.at[2 * i + 3]),
        ]
        for copy in pair:
            copy.start()
        copies.append(pair)
        places.append((act_at, error_at, 0 if i < head else head * chunk))
    rows_copy.wait()
    warm = [two_terms(rows[m]) for m in range(2)]
    grads_copy.wait()
    taken = two_terms(jnp.concatenate([folded(dot(warm[m], grads[m], NT)) for m in range(2)], axis=0))
    wide = 2 * LANES
    for m in range(2):
        grads_t[m * LANES : (m + 1) * LANES] = grads[m].T
    weights = jnp.concatenate([grads_t[...], taken], axis=0)
    first_core = own_matrix() == 0
    step = min(STEP, chunk)
    for i, pair in enumerate(copies):
        act_at, error_at, shift = places[i]
        for copy in pair:
            copy.wait()
        for first in range(i * chunk, (i + 1) * chunk, step):
            here = pl.ds(first - shift, step)
            if i < head:
                part = pl.ds(first, step)
                (high, low), left, turned = transposed_updates(weights, act_at[:, here], [error_at[m, 0, here] for m in range(2)])
                high_ref[:, part] = high
                low_ref[:, part] = low
                moved = [dot(warm[m], turned[m]) for m in range(2)]
            else:
                left = dot(taken, act_at[:, here])
                moved = [dot(warm[m], error_at[m, 0, here], NT) for m in range(2)]
            terms = folded(left) + jnp.concatenate([folded(x) for x in moved], axis=0)
            key, value = terms[:RANK], terms[RANK:]
            keep, send = jnp.where(first_core, key, value), jnp.where(first_core, value, key)
            for b in range(step // LANES):
                keep_ref[first // LANES + b] = keep[:, b * LANES : (b + 1) * LANES]
                send_ref[first // LANES + b] = send[:, b * LANES : (b + 1) * LANES]


def tail_kernel(act_ref, error_ref, grads_t, keep_in, high_in, low_in, high_ref, low_ref, keep_ref):
    keep_ref[...] = keep_in[...]
    count = act_ref.shape[1]
    step = min(STEP, count)
    for first in range(0, count, step):
        here = pl.ds(first, step)
        part = pl.ds(high_ref.shape[1] - count + first, step)
        (high, low), _, _ = transposed_updates(grads_t[...], act_ref[:, here], [error_ref[m, 0, here] for m in range(2)])
        high_ref[:, part] = high
        low_ref[:, part] = low


def make_updates(activations, output_grads, error_feedback, warm_rows):
    tokens, d = activations.shape
    chunk = min(CHUNK, d)
    count = d // chunk
    head = max(1, 3 * count // 4)
    wide, early, late = 2 * LANES, head * chunk, (count - head) * chunk
    loaded = (activations, output_grads, error_feedback, warm_rows)
    tiles = jax.ShapeDtypeStruct((d // LANES, RANK, LANES), F32)
    whole = [pltpu.VMEM((wide, d), BF16)] * 2
    high, low, send, keep, act, errors, grads_t = pl.pallas_call(
        functools.partial(updates_kernel, chunk, head),
        in_specs=[pl.BlockSpec(memory_space=pl.ANY)] * 4,
        out_specs=[WHOLE] * 7,
        out_shape=whole
        + [tiles, tiles, pltpu.VMEM((tokens, late), BF16), pltpu.VMEM((2, 1, late, LANES), BF16), pltpu.VMEM((wide, tokens), BF16)],
        scratch_shapes=[
            pltpu.VMEM((tokens, early), BF16),
            pltpu.VMEM(output_grads.shape, BF16),
            pltpu.VMEM((2, 1, early, LANES), BF16),
            pltpu.VMEM(warm_rows.shape, F32),
            pltpu.SemaphoreType.DMA((2 + 2 * count,)),
        ],
        compiler_params=params(24),
        name="updates",
    )(*map(in_hbm, loaded))
    sent = swapped(send)
    high, low, keep = pl.pallas_call(
        tail_kernel,
        in_specs=[WHOLE] * 6,
        out_specs=[WHOLE] * 3,
        out_shape=whole + [tiles],
        input_output_aliases={4: 0, 5: 1},
        compiler_params=params(8),
        name="updates_tail",
    )(*map(in_vmem, (act, errors, grads_t)), keep, in_vmem(high), in_vmem(low))
    return high, low, added(sent, keep)


def inverse_of_factor(gram):
    row = lax.broadcasted_iota(jnp.int32, (RANK, 2 * RANK), 0)
    column = lax.broadcasted_iota(jnp.int32, (RANK, 2 * RANK), 1)
    table = jnp.concatenate([gram, jnp.zeros_like(gram)], axis=1)
    table = jnp.where(column == row + RANK, jnp.float32(1), table)
    pivots = jnp.zeros((RANK, 2 * RANK), F32)
    for k in range(RANK):
        along = jnp.broadcast_to(table[:, k : k + 1], table.shape)
        pivot = jnp.broadcast_to(along[k : k + 1, :], table.shape)
        pivots = jnp.where(row == k, pivot, pivots)
        table = jnp.where(row > k, table - (along / pivot) * table[k : k + 1, :], table)
    return (table * (1.0 / jnp.sqrt(pivots)))[:, RANK:]


def three_terms(x):
    first, second = split(x)
    return jnp.concatenate([first, second, (x - first.astype(F32) - second.astype(F32)).astype(BF16)], axis=0)


def gram_of(three):
    gram = dot(three, three, NT)
    gram = sum(gram[i * RANK : (i + 1) * RANK] for i in range(3))
    return sum(gram[:, i * RANK : (i + 1) * RANK] for i in range(3))


def right_rows(last, m, three, gram, high_ref, low_ref):
    part = rows_at(m)
    right = folded(dot(three[: 2 * RANK], high_ref[part, :], NT)) + dot(three[:RANK], low_ref[part, :], NT)
    if not last:
        return right
    inverse = inverse_of_factor(gram)
    return exact_dot(exact_dot(inverse, inverse, TN), right)


def right_own_kernel(last, tiles_ref, high_ref, low_ref, out_ref, *gram_ref):
    three = three_terms(rows_of(tiles_ref))
    gram = gram_of(three)
    if not last:
        gram_ref[0][...] = gram
    out_ref[...] = right_rows(last, own_matrix(), three, gram, high_ref, low_ref)


def right_both_kernel(last, mine_ref, tiles_ref, high_ref, low_ref, out_ref):
    own = own_matrix()
    mine = mine_ref[...]
    three = three_terms(rows_of(tiles_ref))
    other = right_rows(last, 1 - own, three, gram_of(three) if last else None, high_ref, low_ref)
    for copy in range(out_ref.shape[0]):
        out_ref[copy, own] = mine
        out_ref[copy, 1 - own] = other


def right_terms(last, copies, tiles, high, low):
    other = swapped(tiles)
    shapes = [jax.ShapeDtypeStruct((RANK, LANES), F32)] + [jax.ShapeDtypeStruct((RANK, RANK), F32)] * (not last)
    mine, *gram = pl.pallas_call(
        functools.partial(right_own_kernel, last),
        in_specs=[WHOLE] * 3,
        out_specs=[WHOLE] * len(shapes),
        out_shape=shapes,
        compiler_params=params(24),
        name="right_own",
    )(tiles, in_vmem(high), in_vmem(low))
    both = pl.pallas_call(
        functools.partial(right_both_kernel, last),
        in_specs=[WHOLE] * 4,
        out_specs=WHOLE,
        out_shape=jax.ShapeDtypeStruct((copies, 2, RANK, LANES), F32),
        compiler_params=params(24),
        name="right_both",
    )(mine, other, in_vmem(high), in_vmem(low))
    return both, other, gram


def total(parts_ref, m):
    return sum(parts_ref[r, m] for r in range(parts_ref.shape[0]))


def left_rows(m, parts_ref, high_ref, low_ref, term_ref):
    part = rows_at(m)
    f_high, f_low = split(total(parts_ref, m))
    both = jnp.concatenate([f_high, f_low], axis=0)
    step = min(2048, high_ref.shape[1])
    for first in range(0, high_ref.shape[1], step):
        columns = pl.ds(first, step)
        terms = folded(dot(both, high_ref[part, columns])) + dot(f_high, low_ref[part, columns])
        for b in range(step // LANES):
            term_ref[first // LANES + b] = terms[:, b * LANES : (b + 1) * LANES]


def left_other_kernel(parts_ref, high_ref, low_ref, term_ref):
    left_rows(1 - own_matrix(), parts_ref, high_ref, low_ref, term_ref)


def left_own_kernel(parts_ref, gram_ref, high_ref, low_ref, term_ref, inverse_ref):
    inverse_ref[...] = inverse_of_factor(gram_ref[...])
    left_rows(own_matrix(), parts_ref, high_ref, low_ref, term_ref)


def add_kernel(x_ref, y_ref, out_ref):
    out_ref[...] = x_ref[...] + y_ref[...]


def added(x, y):
    return pl.pallas_call(
        add_kernel,
        in_specs=[WHOLE] * 2,
        out_specs=WHOLE,
        out_shape=jax.ShapeDtypeStruct(x.shape, F32),
        compiler_params=params(8),
        name="add",
    )(x, y)


def chip_terms(parts, gram, high, low):
    tiles = jax.ShapeDtypeStruct((high.shape[1] // LANES, RANK, LANES), F32)
    high, low = in_vmem(high), in_vmem(low)
    send = pl.pallas_call(
        left_other_kernel,
        in_specs=[WHOLE] * 3,
        out_specs=WHOLE,
        out_shape=tiles,
        compiler_params=params(24),
        name="left_other",
    )(parts, high, low)
    sent = swapped(send)
    keep, inverse = pl.pallas_call(
        left_own_kernel,
        in_specs=[WHOLE] * 4,
        out_specs=[WHOLE] * 2,
        out_shape=[tiles, jax.ShapeDtypeStruct((RANK, RANK), F32)],
        compiler_params=params(24),
        name="left_own",
    )(parts, gram, high, low)
    return added(sent, keep), inverse


def spread_kernel(parts_ref, *rest):
    out_ref = rest[-1]
    total = parts_ref[0]
    for r in range(1, parts_ref.shape[0]):
        total = total + parts_ref[r]
    if len(rest) > 1:
        total = exact_dot(rest[0][...], total)
    for r in range(out_ref.shape[0]):
        out_ref[r] = total


def sum_own(tiles, *inverse):
    parts = lax.all_to_all(tiles, ("dp", "x"), 0, 0)
    spread = pl.pallas_call(
        spread_kernel,
        in_specs=[WHOLE] * (1 + len(inverse)),
        out_specs=WHOLE,
        out_shape=jax.ShapeDtypeStruct(tiles.shape, F32),
        compiler_params=params(8),
        name="spread",
    )(parts, *inverse)
    return lax.all_to_all(spread, ("dp", "x"), 0, 0)


def mean_columns(weights, tiles):
    w_high, w_low = split(weights)
    t_high, t_low = split(tiles)
    left = jnp.concatenate([w_high, w_high, w_low], axis=0)
    right = jnp.concatenate([t_high, t_low, t_high], axis=0)
    return dot(left, right, TN)


def final_kernel(replicas, block, parts_ref, mine_ref, other_ref, high_ref, low_ref, decoded_ref, error_ref, held, decoded, sems):
    weights = [total(parts_ref, m) / replicas for m in range(2)]
    own = own_matrix()

    def mean(m, first, count):
        mine, other = (rows_of(ref, first, count) for ref in (mine_ref, other_ref))
        return mean_columns(weights[m], jnp.where(own == m, mine, other))

    copies = []
    count = high_ref.shape[1] // block
    for i in range(count):
        columns = pl.ds(i * block, block)
        for m in range(2):
            part = pl.ds(m * LANES, LANES)
            updates = high_ref[part, columns].astype(F32) + low_ref[part, columns].astype(F32)
            held[m, 0, columns] = (updates - mean(m, i * block // LANES, block // LANES)).astype(BF16).T
        copies.append(pltpu.make_async_copy(held.at[:, :, columns], error_ref.at[:, :, columns], sems.at[i]))
        copies[-1].start()
        if i == 0:
            tiles = decoded.shape[1] // LANES
            for m in range(2):
                decoded[m] = mean(m, lax.axis_index("dp") * tiles, tiles).T.astype(BF16)
            copies.append(pltpu.make_async_copy(decoded, decoded_ref, sems.at[count]))
            copies[-1].start()
    for copy in copies:
        copy.wait()


def final_outputs(replicas, parts, mine, other, high, low):
    d = high.shape[1]
    block = min(1024, d)
    return pl.pallas_call(
        functools.partial(final_kernel, replicas, block),
        in_specs=[WHOLE] * 5,
        out_specs=[pl.BlockSpec(memory_space=pl.ANY)] * 2,
        out_shape=[
            jax.ShapeDtypeStruct((2, d // replicas, LANES), BF16),
            jax.ShapeDtypeStruct((2, 1, d, LANES), BF16),
        ],
        scratch_shapes=[
            pltpu.VMEM((2, 1, d, LANES), BF16),
            pltpu.VMEM((2, d // replicas, LANES), BF16),
            pltpu.SemaphoreType.DMA((1 + d // block,)),
        ],
        compiler_params=params(24),
        name="final",
    )(parts, mine, other, in_vmem(high), in_vmem(low))


def local(activations, output_grads, error_feedback, warm_start):
    replicas = lax.axis_size("dp")
    high, low, term = make_updates(activations, output_grads, error_feedback, jnp.swapaxes(warm_start, 1, 2))
    terms, _, (gram,) = right_terms(False, replicas, sum_own(term), high, low)
    mine = sum_own(*chip_terms(lax.all_to_all(terms, "dp", 0, 0), gram, high, low))
    terms, other, _ = right_terms(True, replicas, mine, high, low)
    return tuple(final_outputs(replicas, lax.all_to_all(terms, "dp", 0, 0), mine, other, high, low))


def solution(mesh):
    replicas, width = mesh.devices.shape
    split_mesh = Mesh(mesh.devices.reshape(replicas, width // 2, 2), ("dp", "x", "core"))
    tensor = ("x", "core")
    return jax.shard_map(
        local,
        mesh=split_mesh,
        in_specs=(P("dp", None), P(None, "dp", tensor), P(None, "dp", None, tensor), P(None, tensor, None)),
        out_specs=(P(None, "dp", tensor), P(None, "dp", None, tensor)),
        check_vma=False,
    )
```

```python
import functools

import jax
import jax.numpy as jnp
from jax import lax
from jax.experimental import pallas as pl
from jax.experimental.pallas import tpu as pltpu
from jax.sharding import Mesh, PartitionSpec as P

RANK = 8
CHUNK = 1024
STEP = 256
LANES = 128
F32, BF16 = jnp.float32, jnp.bfloat16
HIGHEST = lax.Precision.HIGHEST
NN = (((1,), (0,)), ((), ()))
NT = (((1,), (1,)), ((), ()))
TN = (((0,), (0,)), ((), ()))
WHOLE = pl.BlockSpec(memory_space=pltpu.VMEM)
in_vmem = functools.partial(pltpu.with_memory_space_constraint, memory_space=pltpu.VMEM)
in_hbm = functools.partial(pltpu.with_memory_space_constraint, memory_space=pltpu.HBM)


def params(mebibytes):
    return pltpu.CompilerParams(vmem_limit_bytes=mebibytes << 20)


def split(x):
    high = x.astype(BF16)
    return high, (x - high.astype(F32)).astype(BF16)


def dot(x, y, dims=NN):
    return lax.dot_general(x, y, dims, preferred_element_type=F32)


def exact_dot(x, y, dims=NN):
    return lax.dot_general(x, y, dims, precision=HIGHEST, preferred_element_type=F32)


def two_terms(x):
    return jnp.concatenate(split(x), axis=0)


def folded(pair):
    half = pair.shape[0] // 2
    return pair[:half] + pair[half:]


def rows_of(tiles_ref, first=0, count=None):
    count = tiles_ref.shape[0] if count is None else count
    return jnp.concatenate([tiles_ref[first + b] for b in range(count)], axis=1)


def own_matrix():
    return lax.axis_index("core")


def swapped(x):
    return lax.ppermute(x, "core", [(0, 1), (1, 0)])


def rows_at(m):
    return pl.ds(pl.multiple_of(m * LANES, LANES), LANES)


def transposed_updates(weights, act, errors):
    products = dot(weights, act)
    turned = [e.T for e in errors]
    wide = 2 * LANES
    return split(products[:wide] + jnp.concatenate(turned, axis=0).astype(F32)), products[wide:], turned


def updates_kernel(chunk, head, act_ref, grads_ref, error_ref, rows_ref, high_ref, low_ref, send_ref, keep_ref, tail_act, tail_errors, grads_t, act, grads, errors, rows, sems):
    d = high_ref.shape[1]
    rows_copy = pltpu.make_async_copy(rows_ref, rows, sems.at[0])
    grads_copy = pltpu.make_async_copy(grads_ref, grads, sems.at[1])
    rows_copy.start()
    grads_copy.start()
    places, copies = [], []
    for i in range(d // chunk):
        part = pl.ds(i * chunk, chunk)
        here = part if i < head else pl.ds((i - head) * chunk, chunk)
        act_at, error_at = (act, errors) if i < head else (tail_act, tail_errors)
        pair = [
            pltpu.make_async_copy(error_ref.at[:, :, part], error_at.at[:, :, here], sems.at[2 * i + 2]),
            pltpu.make_async_copy(act_ref.at[:, part], act_at.at[:, here], sems.at[2 * i + 3]),
        ]
        for copy in pair:
            copy.start()
        copies.append(pair)
        places.append((act_at, error_at, 0 if i < head else head * chunk))
    rows_copy.wait()
    warm = [two_terms(rows[m]) for m in range(2)]
    grads_copy.wait()
    taken = two_terms(jnp.concatenate([folded(dot(warm[m], grads[m], NT)) for m in range(2)], axis=0))
    wide = 2 * LANES
    for m in range(2):
        grads_t[m * LANES : (m + 1) * LANES] = grads[m].T
    weights = jnp.concatenate([grads_t[...], taken], axis=0)
    first_core = own_matrix() == 0
    step = min(STEP, chunk)
    for i, pair in enumerate(copies):
        act_at, error_at, shift = places[i]
        pair[0].wait()
        if i >= head:
            every = pl.ds(i * chunk - shift, chunk)
            ahead = [dot(warm[m], error_at[m, 0, every], NT) for m in range(2)]
        pair[1].wait()
        for first in range(i * chunk, (i + 1) * chunk, step):
            here = pl.ds(first - shift, step)
            if i < head:
                part = pl.ds(first, step)
                (high, low), left, turned = transposed_updates(weights, act_at[:, here], [error_at[m, 0, here] for m in range(2)])
                high_ref[:, part] = high
                low_ref[:, part] = low
                moved = [dot(warm[m], turned[m]) for m in range(2)]
            else:
                left = dot(taken, act_at[:, here])
                moved = [x[:, first - i * chunk : first - i * chunk + step] for x in ahead]
            terms = folded(left) + jnp.concatenate([folded(x) for x in moved], axis=0)
            key, value = terms[:RANK], terms[RANK:]
            keep, send = jnp.where(first_core, key, value), jnp.where(first_core, value, key)
            for b in range(step // LANES):
                keep_ref[first // LANES + b] = keep[:, b * LANES : (b + 1) * LANES]
                send_ref[first // LANES + b] = send[:, b * LANES : (b + 1) * LANES]


def tail_kernel(act_ref, error_ref, grads_t, keep_in, high_in, low_in, high_ref, low_ref, keep_ref):
    keep_ref[...] = keep_in[...]
    count = act_ref.shape[1]
    step = min(STEP, count)
    for first in range(0, count, step):
        here = pl.ds(first, step)
        part = pl.ds(high_ref.shape[1] - count + first, step)
        (high, low), _, _ = transposed_updates(grads_t[...], act_ref[:, here], [error_ref[m, 0, here] for m in range(2)])
        high_ref[:, part] = high
        low_ref[:, part] = low


def make_updates(activations, output_grads, error_feedback, warm_rows):
    tokens, d = activations.shape
    chunk = min(CHUNK, d)
    count = d // chunk
    head = max(1, 3 * count // 4)
    wide, early, late = 2 * LANES, head * chunk, (count - head) * chunk
    loaded = (activations, output_grads, error_feedback, warm_rows)
    tiles = jax.ShapeDtypeStruct((d // LANES, RANK, LANES), F32)
    whole = [pltpu.VMEM((wide, d), BF16)] * 2
    high, low, send, keep, act, errors, grads_t = pl.pallas_call(
        functools.partial(updates_kernel, chunk, head),
        in_specs=[pl.BlockSpec(memory_space=pl.ANY)] * 4,
        out_specs=[WHOLE] * 7,
        out_shape=whole
        + [tiles, tiles, pltpu.VMEM((tokens, late), BF16), pltpu.VMEM((2, 1, late, LANES), BF16), pltpu.VMEM((wide, tokens), BF16)],
        scratch_shapes=[
            pltpu.VMEM((tokens, early), BF16),
            pltpu.VMEM(output_grads.shape, BF16),
            pltpu.VMEM((2, 1, early, LANES), BF16),
            pltpu.VMEM(warm_rows.shape, F32),
            pltpu.SemaphoreType.DMA((2 + 2 * count,)),
        ],
        compiler_params=params(24),
        name="updates",
    )(*map(in_hbm, loaded))
    sent = swapped(send)
    high, low, keep = pl.pallas_call(
        tail_kernel,
        in_specs=[WHOLE] * 6,
        out_specs=[WHOLE] * 3,
        out_shape=whole + [tiles],
        input_output_aliases={4: 0, 5: 1},
        compiler_params=params(8),
        name="updates_tail",
    )(*map(in_vmem, (act, errors, grads_t)), keep, in_vmem(high), in_vmem(low))
    return high, low, added(sent, keep)


def inverse_of_factor(gram):
    row = lax.broadcasted_iota(jnp.int32, (RANK, 2 * RANK), 0)
    column = lax.broadcasted_iota(jnp.int32, (RANK, 2 * RANK), 1)
    table = jnp.concatenate([gram, jnp.zeros_like(gram)], axis=1)
    table = jnp.where(column == row + RANK, jnp.float32(1), table)
    pivots = jnp.zeros((RANK, 2 * RANK), F32)
    for k in range(RANK):
        along = jnp.broadcast_to(table[:, k : k + 1], table.shape)
        pivot = jnp.broadcast_to(along[k : k + 1, :], table.shape)
        pivots = jnp.where(row == k, pivot, pivots)
        table = jnp.where(row > k, table - (along / pivot) * table[k : k + 1, :], table)
    return (table * (1.0 / jnp.sqrt(pivots)))[:, RANK:]


def three_terms(x):
    first, second = split(x)
    return jnp.concatenate([first, second, (x - first.astype(F32) - second.astype(F32)).astype(BF16)], axis=0)


def gram_of(three):
    gram = dot(three, three, NT)
    gram = sum(gram[i * RANK : (i + 1) * RANK] for i in range(3))
    return sum(gram[:, i * RANK : (i + 1) * RANK] for i in range(3))


def right_rows(m, three, high_ref, low_ref):
    part = rows_at(m)
    return folded(dot(three[: 2 * RANK], high_ref[part, :], NT)) + dot(three[:RANK], low_ref[part, :], NT)


def inverse_of_gram(gram):
    inverse = inverse_of_factor(gram)
    return exact_dot(inverse, inverse, TN)


def right_own_kernel(last, tiles_ref, high_ref, low_ref, out_ref, norm_ref):
    three = three_terms(rows_of(tiles_ref))
    gram = gram_of(three)
    out_ref[...] = right_rows(own_matrix(), three, high_ref, low_ref)
    norm_ref[...] = inverse_of_gram(gram) if last else gram


def right_both_kernel(last, mine_ref, tiles_ref, high_ref, low_ref, out_ref, *norm_ref):
    own = own_matrix()
    mine = mine_ref[...]
    three = three_terms(rows_of(tiles_ref))
    if last:
        gram = gram_of(three)
    other = right_rows(1 - own, three, high_ref, low_ref)
    for copy in range(out_ref.shape[0]):
        out_ref[copy, own] = mine
        out_ref[copy, 1 - own] = other
    if last:
        norm_ref[0][...] = inverse_of_gram(gram)


def right_terms(last, copies, tiles, high, low):
    other = swapped(tiles)
    norm = jax.ShapeDtypeStruct((RANK, RANK), F32)
    mine, own_norm = pl.pallas_call(
        functools.partial(right_own_kernel, last),
        in_specs=[WHOLE] * 3,
        out_specs=[WHOLE] * 2,
        out_shape=[jax.ShapeDtypeStruct((RANK, LANES), F32), norm],
        compiler_params=params(24),
        name="right_own",
    )(tiles, in_vmem(high), in_vmem(low))
    shapes = [jax.ShapeDtypeStruct((copies, 2, RANK, LANES), F32)] + [norm] * last
    both, *other_norm = pl.pallas_call(
        functools.partial(right_both_kernel, last),
        in_specs=[WHOLE] * 4,
        out_specs=[WHOLE] * len(shapes),
        out_shape=shapes,
        compiler_params=params(24),
        name="right_both",
    )(mine, other, in_vmem(high), in_vmem(low))
    return both, other, [own_norm] + other_norm


def total(parts_ref, m):
    return sum(parts_ref[r, m] for r in range(parts_ref.shape[0]))


def left_rows(m, parts_ref, high_ref, low_ref, term_ref):
    part = rows_at(m)
    f_high, f_low = split(total(parts_ref, m))
    both = jnp.concatenate([f_high, f_low], axis=0)
    step = min(2048, high_ref.shape[1])
    for first in range(0, high_ref.shape[1], step):
        columns = pl.ds(first, step)
        terms = folded(dot(both, high_ref[part, columns])) + dot(f_high, low_ref[part, columns])
        for b in range(step // LANES):
            term_ref[first // LANES + b] = terms[:, b * LANES : (b + 1) * LANES]


def left_other_kernel(parts_ref, high_ref, low_ref, term_ref):
    left_rows(1 - own_matrix(), parts_ref, high_ref, low_ref, term_ref)


def left_own_kernel(parts_ref, gram_ref, high_ref, low_ref, term_ref, inverse_ref):
    inverse_ref[...] = inverse_of_factor(gram_ref[...])
    left_rows(own_matrix(), parts_ref, high_ref, low_ref, term_ref)


def add_kernel(x_ref, y_ref, out_ref):
    out_ref[...] = x_ref[...] + y_ref[...]


def added(x, y):
    return pl.pallas_call(
        add_kernel,
        in_specs=[WHOLE] * 2,
        out_specs=WHOLE,
        out_shape=jax.ShapeDtypeStruct(x.shape, F32),
        compiler_params=params(8),
        name="add",
    )(x, y)


def chip_terms(parts, gram, high, low):
    tiles = jax.ShapeDtypeStruct((high.shape[1] // LANES, RANK, LANES), F32)
    high, low = in_vmem(high), in_vmem(low)
    send = pl.pallas_call(
        left_other_kernel,
        in_specs=[WHOLE] * 3,
        out_specs=WHOLE,
        out_shape=tiles,
        compiler_params=params(24),
        name="left_other",
    )(parts, high, low)
    sent = swapped(send)
    keep, inverse = pl.pallas_call(
        left_own_kernel,
        in_specs=[WHOLE] * 4,
        out_specs=[WHOLE] * 2,
        out_shape=[tiles, jax.ShapeDtypeStruct((RANK, RANK), F32)],
        compiler_params=params(24),
        name="left_own",
    )(parts, gram, high, low)
    return added(sent, keep), inverse


def spread_kernel(parts_ref, *rest):
    out_ref = rest[-1]
    total = parts_ref[0]
    for r in range(1, parts_ref.shape[0]):
        total = total + parts_ref[r]
    if len(rest) > 1:
        total = exact_dot(rest[0][...], total)
    for r in range(out_ref.shape[0]):
        out_ref[r] = total


def sum_own(tiles, *inverse):
    parts = lax.all_to_all(tiles, ("dp", "x"), 0, 0)
    spread = pl.pallas_call(
        spread_kernel,
        in_specs=[WHOLE] * (1 + len(inverse)),
        out_specs=WHOLE,
        out_shape=jax.ShapeDtypeStruct(tiles.shape, F32),
        compiler_params=params(8),
        name="spread",
    )(parts, *inverse)
    return lax.all_to_all(spread, ("dp", "x"), 0, 0)


def mean_columns(weights, tiles):
    w_high, w_low = split(weights)
    t_high, t_low = split(tiles)
    left = jnp.concatenate([w_high, w_high, w_low], axis=0)
    right = jnp.concatenate([t_high, t_low, t_high], axis=0)
    return dot(left, right, TN)


def final_kernel(replicas, block, parts_ref, mine_ref, other_ref, own_norm, other_norm, high_ref, low_ref, decoded_ref, error_ref, held, decoded, sems):
    own = own_matrix()
    norms = [jnp.where(own == m, own_norm[...], other_norm[...]) for m in range(2)]
    weights = [exact_dot(norms[m], total(parts_ref, m)) / replicas for m in range(2)]

    def mean(m, first, count):
        mine, other = (rows_of(ref, first, count) for ref in (mine_ref, other_ref))
        return mean_columns(weights[m], jnp.where(own == m, mine, other))

    copies = []
    d = high_ref.shape[1]
    starts = list(range(0, d, block)) + [d - block // 2]
    count = len(starts)
    for i, (first, end) in enumerate(zip(starts, starts[1:] + [d])):
        columns = pl.ds(first, end - first)
        for m in range(2):
            part = pl.ds(m * LANES, LANES)
            updates = high_ref[part, columns].astype(F32) + low_ref[part, columns].astype(F32)
            held[m, 0, columns] = (updates - mean(m, first // LANES, (end - first) // LANES)).astype(BF16).T
        copies.append(pltpu.make_async_copy(held.at[:, :, columns], error_ref.at[:, :, columns], sems.at[i]))
        copies[-1].start()
        if i == 0:
            tiles = decoded.shape[1] // LANES
            for m in range(2):
                decoded[m] = mean(m, lax.axis_index("dp") * tiles, tiles).T.astype(BF16)
            copies.append(pltpu.make_async_copy(decoded, decoded_ref, sems.at[count]))
            copies[-1].start()
    for copy in copies:
        copy.wait()


def final_outputs(replicas, parts, mine, other, norms, high, low):
    d = high.shape[1]
    block = min(1024, d)
    return pl.pallas_call(
        functools.partial(final_kernel, replicas, block),
        in_specs=[WHOLE] * 7,
        out_specs=[pl.BlockSpec(memory_space=pl.ANY)] * 2,
        out_shape=[
            jax.ShapeDtypeStruct((2, d // replicas, LANES), BF16),
            jax.ShapeDtypeStruct((2, 1, d, LANES), BF16),
        ],
        scratch_shapes=[
            pltpu.VMEM((2, 1, d, LANES), BF16),
            pltpu.VMEM((2, d // replicas, LANES), BF16),
            pltpu.SemaphoreType.DMA((2 + d // block,)),
        ],
        compiler_params=params(24),
        name="final",
    )(parts, mine, other, *norms, in_vmem(high), in_vmem(low))


def local(activations, output_grads, error_feedback, warm_start):
    replicas = lax.axis_size("dp")
    high, low, term = make_updates(activations, output_grads, error_feedback, jnp.swapaxes(warm_start, 1, 2))
    terms, _, (gram,) = right_terms(False, replicas, sum_own(term), high, low)
    mine = sum_own(*chip_terms(lax.all_to_all(terms, "dp", 0, 0), gram, high, low))
    terms, other, norms = right_terms(True, replicas, mine, high, low)
    return tuple(final_outputs(replicas, lax.all_to_all(terms, "dp", 0, 0), mine, other, norms, high, low))


def solution(mesh):
    replicas, width = mesh.devices.shape
    split_mesh = Mesh(mesh.devices.reshape(replicas, width // 2, 2), ("dp", "x", "core"))
    tensor = ("x", "core")
    return jax.shard_map(
        local,
        mesh=split_mesh,
        in_specs=(P("dp", None), P(None, "dp", tensor), P(None, "dp", None, tensor), P(None, tensor, None)),
        out_specs=(P(None, "dp", tensor), P(None, "dp", None, tensor)),
        check_vma=False,
    )
```

```python
import functools

import jax
import jax.numpy as jnp
from jax import lax
from jax.experimental import pallas as pl
from jax.experimental.pallas import tpu as pltpu
from jax.sharding import Mesh, PartitionSpec as P

RANK = 8
CHUNK = 1024
STEP = 256
LANES = 128
F32, BF16 = jnp.float32, jnp.bfloat16
HIGHEST = lax.Precision.HIGHEST
NN = (((1,), (0,)), ((), ()))
NT = (((1,), (1,)), ((), ()))
TN = (((0,), (0,)), ((), ()))
WHOLE = pl.BlockSpec(memory_space=pltpu.VMEM)
in_vmem = functools.partial(pltpu.with_memory_space_constraint, memory_space=pltpu.VMEM)
in_hbm = functools.partial(pltpu.with_memory_space_constraint, memory_space=pltpu.HBM)


def params(mebibytes):
    return pltpu.CompilerParams(vmem_limit_bytes=mebibytes << 20)


def split(x):
    high = x.astype(BF16)
    return high, (x - high.astype(F32)).astype(BF16)


def dot(x, y, dims=NN):
    return lax.dot_general(x, y, dims, preferred_element_type=F32)


def exact_dot(x, y, dims=NN):
    return lax.dot_general(x, y, dims, precision=HIGHEST, preferred_element_type=F32)


def two_terms(x):
    return jnp.concatenate(split(x), axis=0)


def folded(pair):
    half = pair.shape[0] // 2
    return pair[:half] + pair[half:]


def rows_of(tiles_ref, first=0, count=None):
    count = tiles_ref.shape[0] if count is None else count
    return jnp.concatenate([tiles_ref[first + b] for b in range(count)], axis=1)


def own_matrix():
    return lax.axis_index("core")


def swapped(x):
    return lax.ppermute(x, "core", [(0, 1), (1, 0)])


def rows_at(m):
    return pl.ds(pl.multiple_of(m * LANES, LANES), LANES)


def transposed_updates(weights, act, errors):
    products = dot(weights, act)
    turned = [e.T for e in errors]
    wide = 2 * LANES
    return split(products[:wide] + jnp.concatenate(turned, axis=0).astype(F32)), products[wide:], turned


def updates_kernel(chunk, head, act_ref, grads_ref, error_ref, rows_ref, high_ref, low_ref, send_ref, keep_ref, tail_act, tail_errors, grads_t, act, grads, errors, rows, sems):
    d = high_ref.shape[1]
    rows_copy = pltpu.make_async_copy(rows_ref, rows, sems.at[0])
    grads_copy = pltpu.make_async_copy(grads_ref, grads, sems.at[1])
    rows_copy.start()
    grads_copy.start()
    places, copies = [], []
    for i in range(d // chunk):
        part = pl.ds(i * chunk, chunk)
        here = part if i < head else pl.ds((i - head) * chunk, chunk)
        act_at, error_at = (act, errors) if i < head else (tail_act, tail_errors)
        pair = [
            pltpu.make_async_copy(act_ref.at[:, part], act_at.at[:, here], sems.at[2 * i + 2]),
            pltpu.make_async_copy(error_ref.at[:, :, part], error_at.at[:, :, here], sems.at[2 * i + 3]),
        ]
        for copy in pair:
            copy.start()
        copies.append(pair)
        places.append((act_at, error_at, 0 if i < head else head * chunk))
    rows_copy.wait()
    warm = [two_terms(rows[m]) for m in range(2)]
    grads_copy.wait()
    taken = two_terms(jnp.concatenate([folded(dot(warm[m], grads[m], NT)) for m in range(2)], axis=0))
    wide = 2 * LANES
    for m in range(2):
        grads_t[m * LANES : (m + 1) * LANES] = grads[m].T
    weights = jnp.concatenate([grads_t[...], taken], axis=0)
    first_core = own_matrix() == 0
    step = min(STEP, chunk)
    for i, pair in enumerate(copies):
        act_at, error_at, shift = places[i]
        for copy in pair:
            copy.wait()
        for first in range(i * chunk, (i + 1) * chunk, step):
            here = pl.ds(first - shift, step)
            if i < head:
                part = pl.ds(first, step)
                (high, low), left, turned = transposed_updates(weights, act_at[:, here], [error_at[m, 0, here] for m in range(2)])
                high_ref[:, part] = high
                low_ref[:, part] = low
                moved = [dot(warm[m], turned[m]) for m in range(2)]
            else:
                left = dot(taken, act_at[:, here])
                moved = [dot(warm[m], error_at[m, 0, here], NT) for m in range(2)]
            terms = folded(left) + jnp.concatenate([folded(x) for x in moved], axis=0)
            key, value = terms[:RANK], terms[RANK:]
            keep, send = jnp.where(first_core, key, value), jnp.where(first_core, value, key)
            for b in range(step // LANES):
                keep_ref[first // LANES + b] = keep[:, b * LANES : (b + 1) * LANES]
                send_ref[first // LANES + b] = send[:, b * LANES : (b + 1) * LANES]


def tail_kernel(act_ref, error_ref, grads_t, keep_in, high_in, low_in, high_ref, low_ref, keep_ref):
    keep_ref[...] = keep_in[...]
    count = act_ref.shape[1]
    step = min(STEP, count)
    for first in range(0, count, step):
        here = pl.ds(first, step)
        part = pl.ds(high_ref.shape[1] - count + first, step)
        (high, low), _, _ = transposed_updates(grads_t[...], act_ref[:, here], [error_ref[m, 0, here] for m in range(2)])
        high_ref[:, part] = high
        low_ref[:, part] = low


def make_updates(activations, output_grads, error_feedback, warm_rows):
    tokens, d = activations.shape
    chunk = min(CHUNK, d)
    count = d // chunk
    head = max(1, 3 * count // 4)
    wide, early, late = 2 * LANES, head * chunk, (count - head) * chunk
    loaded = (activations, output_grads, error_feedback, warm_rows)
    tiles = jax.ShapeDtypeStruct((d // LANES, RANK, LANES), F32)
    whole = [pltpu.VMEM((wide, d), BF16)] * 2
    high, low, send, keep, act, errors, grads_t = pl.pallas_call(
        functools.partial(updates_kernel, chunk, head),
        in_specs=[pl.BlockSpec(memory_space=pl.ANY)] * 4,
        out_specs=[WHOLE] * 7,
        out_shape=whole
        + [tiles, tiles, pltpu.VMEM((tokens, late), BF16), pltpu.VMEM((2, 1, late, LANES), BF16), pltpu.VMEM((wide, tokens), BF16)],
        scratch_shapes=[
            pltpu.VMEM((tokens, early), BF16),
            pltpu.VMEM(output_grads.shape, BF16),
            pltpu.VMEM((2, 1, early, LANES), BF16),
            pltpu.VMEM(warm_rows.shape, F32),
            pltpu.SemaphoreType.DMA((2 + 2 * count,)),
        ],
        compiler_params=params(24),
        name="updates",
    )(*map(in_hbm, loaded))
    sent = swapped(send)
    high, low, keep = pl.pallas_call(
        tail_kernel,
        in_specs=[WHOLE] * 6,
        out_specs=[WHOLE] * 3,
        out_shape=whole + [tiles],
        input_output_aliases={4: 0, 5: 1},
        compiler_params=params(8),
        name="updates_tail",
    )(*map(in_vmem, (act, errors, grads_t)), keep, in_vmem(high), in_vmem(low))
    return high, low, added(sent, keep)


def inverse_of_factor(gram):
    row = lax.broadcasted_iota(jnp.int32, (RANK, 2 * RANK), 0)
    column = lax.broadcasted_iota(jnp.int32, (RANK, 2 * RANK), 1)
    table = jnp.concatenate([gram, jnp.zeros_like(gram)], axis=1)
    table = jnp.where(column == row + RANK, jnp.float32(1), table)
    pivots = jnp.zeros((RANK, 2 * RANK), F32)
    for k in range(RANK):
        along = jnp.broadcast_to(table[:, k : k + 1], table.shape)
        pivot = jnp.broadcast_to(along[k : k + 1, :], table.shape)
        pivots = jnp.where(row == k, pivot, pivots)
        table = jnp.where(row > k, table - (along / pivot) * table[k : k + 1, :], table)
    return (table * (1.0 / jnp.sqrt(pivots)))[:, RANK:]


def three_terms(x):
    first, second = split(x)
    return jnp.concatenate([first, second, (x - first.astype(F32) - second.astype(F32)).astype(BF16)], axis=0)


def gram_of(three):
    gram = dot(three, three, NT)
    gram = sum(gram[i * RANK : (i + 1) * RANK] for i in range(3))
    return sum(gram[:, i * RANK : (i + 1) * RANK] for i in range(3))


def right_rows(m, three, high_ref, low_ref):
    part = rows_at(m)
    return folded(dot(three[: 2 * RANK], high_ref[part, :], NT)) + dot(three[:RANK], low_ref[part, :], NT)


def inverse_of_gram(gram):
    inverse = inverse_of_factor(gram)
    return exact_dot(inverse, inverse, TN)


def right_own_kernel(last, tiles_ref, high_ref, low_ref, out_ref, norm_ref):
    three = three_terms(rows_of(tiles_ref))
    gram = gram_of(three)
    out_ref[...] = right_rows(own_matrix(), three, high_ref, low_ref)
    norm_ref[...] = inverse_of_gram(gram) if last else gram


def right_both_kernel(last, mine_ref, tiles_ref, high_ref, low_ref, out_ref, *norm_ref):
    own = own_matrix()
    mine = mine_ref[...]
    three = three_terms(rows_of(tiles_ref))
    if last:
        gram = gram_of(three)
    other = right_rows(1 - own, three, high_ref, low_ref)
    for copy in range(out_ref.shape[0]):
        out_ref[copy, own] = mine
        out_ref[copy, 1 - own] = other
    if last:
        norm_ref[0][...] = inverse_of_gram(gram)


def right_terms(last, copies, tiles, high, low):
    other = swapped(tiles)
    norm = jax.ShapeDtypeStruct((RANK, RANK), F32)
    mine, own_norm = pl.pallas_call(
        functools.partial(right_own_kernel, last),
        in_specs=[WHOLE] * 3,
        out_specs=[WHOLE] * 2,
        out_shape=[jax.ShapeDtypeStruct((RANK, LANES), F32), norm],
        compiler_params=params(24),
        name="right_own",
    )(tiles, in_vmem(high), in_vmem(low))
    shapes = [jax.ShapeDtypeStruct((copies, 2, RANK, LANES), F32)] + [norm] * last
    both, *other_norm = pl.pallas_call(
        functools.partial(right_both_kernel, last),
        in_specs=[WHOLE] * 4,
        out_specs=[WHOLE] * len(shapes),
        out_shape=shapes,
        compiler_params=params(24),
        name="right_both",
    )(mine, other, in_vmem(high), in_vmem(low))
    return both, other, [own_norm] + other_norm


def total(parts_ref, m):
    return sum(parts_ref[r, m] for r in range(parts_ref.shape[0]))


def left_rows(m, parts_ref, high_ref, low_ref, term_ref):
    part = rows_at(m)
    f_high, f_low = split(total(parts_ref, m))
    both = jnp.concatenate([f_high, f_low], axis=0)
    step = min(2048, high_ref.shape[1])
    for first in range(0, high_ref.shape[1], step):
        columns = pl.ds(first, step)
        terms = folded(dot(both, high_ref[part, columns])) + dot(f_high, low_ref[part, columns])
        for b in range(step // LANES):
            term_ref[first // LANES + b] = terms[:, b * LANES : (b + 1) * LANES]


def left_other_kernel(parts_ref, high_ref, low_ref, term_ref):
    left_rows(1 - own_matrix(), parts_ref, high_ref, low_ref, term_ref)


def left_own_kernel(parts_ref, gram_ref, high_ref, low_ref, term_ref, inverse_ref):
    inverse_ref[...] = inverse_of_factor(gram_ref[...])
    left_rows(own_matrix(), parts_ref, high_ref, low_ref, term_ref)


def add_kernel(x_ref, y_ref, out_ref):
    out_ref[...] = x_ref[...] + y_ref[...]


def added(x, y):
    return pl.pallas_call(
        add_kernel,
        in_specs=[WHOLE] * 2,
        out_specs=WHOLE,
        out_shape=jax.ShapeDtypeStruct(x.shape, F32),
        compiler_params=params(8),
        name="add",
    )(x, y)


def chip_terms(parts, gram, high, low):
    tiles = jax.ShapeDtypeStruct((high.shape[1] // LANES, RANK, LANES), F32)
    high, low = in_vmem(high), in_vmem(low)
    send = pl.pallas_call(
        left_other_kernel,
        in_specs=[WHOLE] * 3,
        out_specs=WHOLE,
        out_shape=tiles,
        compiler_params=params(24),
        name="left_other",
    )(parts, high, low)
    sent = swapped(send)
    keep, inverse = pl.pallas_call(
        left_own_kernel,
        in_specs=[WHOLE] * 4,
        out_specs=[WHOLE] * 2,
        out_shape=[tiles, jax.ShapeDtypeStruct((RANK, RANK), F32)],
        compiler_params=params(24),
        name="left_own",
    )(parts, gram, high, low)
    return added(sent, keep), inverse


def spread_kernel(parts_ref, *rest):
    out_ref = rest[-1]
    total = parts_ref[0]
    for r in range(1, parts_ref.shape[0]):
        total = total + parts_ref[r]
    if len(rest) > 1:
        total = exact_dot(rest[0][...], total)
    for r in range(out_ref.shape[0]):
        out_ref[r] = total


def sum_own(tiles, *inverse):
    parts = lax.all_to_all(tiles, ("dp", "x"), 0, 0)
    spread = pl.pallas_call(
        spread_kernel,
        in_specs=[WHOLE] * (1 + len(inverse)),
        out_specs=WHOLE,
        out_shape=jax.ShapeDtypeStruct(tiles.shape, F32),
        compiler_params=params(8),
        name="spread",
    )(parts, *inverse)
    return lax.all_to_all(spread, ("dp", "x"), 0, 0)


def mean_columns(weights, tiles):
    w_high, w_low = split(weights)
    t_high, t_low = split(tiles)
    left = jnp.concatenate([w_high, w_high, w_low], axis=0)
    right = jnp.concatenate([t_high, t_low, t_high], axis=0)
    return dot(left, right, TN)


def final_kernel(replicas, block, parts_ref, mine_ref, other_ref, own_norm, other_norm, high_ref, low_ref, decoded_ref, error_ref, held, decoded, sems):
    own = own_matrix()
    norms = [jnp.where(own == m, own_norm[...], other_norm[...]) for m in range(2)]
    weights = [exact_dot(norms[m], total(parts_ref, m)) / replicas for m in range(2)]

    def mean(m, first, count):
        mine, other = (rows_of(ref, first, count) for ref in (mine_ref, other_ref))
        return mean_columns(weights[m], jnp.where(own == m, mine, other))

    copies = []
    d = high_ref.shape[1]
    count = d // block
    for i, first in enumerate(range(0, d, block)):
        columns = pl.ds(first, block)
        for m in range(2):
            part = pl.ds(m * LANES, LANES)
            updates = high_ref[part, columns].astype(F32) + low_ref[part, columns].astype(F32)
            held[m, 0, columns] = (updates - mean(m, first // LANES, block // LANES)).astype(BF16).T
        copies.append(pltpu.make_async_copy(held.at[:, :, columns], error_ref.at[:, :, columns], sems.at[i]))
        copies[-1].start()
        if i == 0:
            tiles = decoded.shape[1] // LANES
            for m in range(2):
                decoded[m] = mean(m, lax.axis_index("dp") * tiles, tiles).T.astype(BF16)
            copies.append(pltpu.make_async_copy(decoded, decoded_ref, sems.at[count]))
            copies[-1].start()
    for copy in copies:
        copy.wait()


def final_outputs(replicas, parts, mine, other, norms, high, low):
    d = high.shape[1]
    block = min(1024, d)
    return pl.pallas_call(
        functools.partial(final_kernel, replicas, block),
        in_specs=[WHOLE] * 7,
        out_specs=[pl.BlockSpec(memory_space=pl.ANY)] * 2,
        out_shape=[
            jax.ShapeDtypeStruct((2, d // replicas, LANES), BF16),
            jax.ShapeDtypeStruct((2, 1, d, LANES), BF16),
        ],
        scratch_shapes=[
            pltpu.VMEM((2, 1, d, LANES), BF16),
            pltpu.VMEM((2, d // replicas, LANES), BF16),
            pltpu.SemaphoreType.DMA((1 + d // block,)),
        ],
        compiler_params=params(24),
        name="final",
    )(parts, mine, other, *norms, in_vmem(high), in_vmem(low))


def local(activations, output_grads, error_feedback, warm_start):
    replicas = lax.axis_size("dp")
    high, low, term = make_updates(activations, output_grads, error_feedback, jnp.swapaxes(warm_start, 1, 2))
    terms, _, (gram,) = right_terms(False, replicas, sum_own(term), high, low)
    mine = sum_own(*chip_terms(lax.all_to_all(terms, "dp", 0, 0), gram, high, low))
    terms, other, norms = right_terms(True, replicas, mine, high, low)
    return tuple(final_outputs(replicas, lax.all_to_all(terms, "dp", 0, 0), mine, other, norms, high, low))


def solution(mesh):
    replicas, width = mesh.devices.shape
    split_mesh = Mesh(mesh.devices.reshape(replicas, width // 2, 2), ("dp", "x", "core"))
    tensor = ("x", "core")
    return jax.shard_map(
        local,
        mesh=split_mesh,
        in_specs=(P("dp", None), P(None, "dp", tensor), P(None, "dp", None, tensor), P(None, tensor, None)),
        out_specs=(P(None, "dp", tensor), P(None, "dp", None, tensor)),
        check_vma=False,
    )
```
